32 devices in a mesh: lag: 4 (over x, core), row: 8 (over z, y).
Axes of the slice: x: 2, y: 2, z: 4, core: 2. Of those that a mesh axis runs over, the one named last changes fastest.
Arguments:
- currents: bfloat16 [512, 4096], P('lag', 'row'), may hold values from -6 to 6
- panels: bfloat16 [4, 4096, 4096], P('lag', 'row'), may hold values from -0.09375 to 0.09375
- excitation: float32 [512, 4096], P('lag', 'row'), may hold values from -6 to 6
Outputs:
- residual: float32 [512, 4096], P('lag', 'row')
The draws below stay inside these ranges and needn't reach their ends.
All inputs are finite; a program needn't handle non-finite values.
Results may differ from the reference program's by a relative error of at most 0.0003.
Values may be sent and summed in bfloat16 or wider, within the bound.
A program may use at most 64 MiB of HBM per device.

```python
import jax
import jax.numpy as jnp
from jax import lax

N = 4096
LAGS = 4
TIMES = 512


def level_of(key, shape, shards, low, largest):
    def one(position, blocks):
        steps = jax.random.uniform(jax.random.fold_in(jax.random.fold_in(key, 6), position), (blocks,), jnp.float32, low / len(shards), largest / len(shards))
        return jnp.repeat(jnp.exp(steps), shape[position] // blocks).reshape((-1,) + (1,) * (len(shape) - position - 1))

    loudness = one(*shards[0])
    for cut in shards[1:]:
        loudness = loudness * one(*cut)
    return loudness


def centred(stream_key, shape, deviation, bound, cuts=(), kind=jnp.bfloat16):
    factor_of = level_of(stream_key, shape, cuts, -0.22, 0.18) if cuts else 1.0
    drawn = jax.random.normal(stream_key, shape, jnp.float32) * deviation * factor_of
    return jnp.minimum(jnp.maximum(drawn, -bound), bound).astype(kind)


def setup_inputs(seed: int = 0) -> dict:
    keys = jax.random.split(jax.random.key(seed), 4)
    currents = centred(keys[0], (TIMES, N), 1.0, 6.0, ((0, 4), (1, 8)))
    panels = centred(keys[1], (LAGS, N, N), N ** -0.5, 0.09375, ((0, 4), (1, 8)))
    excitation = centred(keys[2], (TIMES, N), 1.0, 6.0, ((0, 4), (1, 8)), jnp.float32)
    return {"currents": currents, "panels": panels, "excitation": excitation}


def reference(currents, panels, excitation):
    padded = jnp.concatenate([jnp.zeros((LAGS - 1, N), jnp.bfloat16), currents], 0)

    def add_term(running, k):
        shifted = lax.dynamic_slice_in_dim(padded, (LAGS - 1 - k).astype(jnp.int32), TIMES, 0)
        matrix = lax.dynamic_index_in_dim(panels, k.astype(jnp.int32), 0, keepdims=False)
        product = lax.dot_general(shifted, matrix, (((1,), (1,)), ((), ())), preferred_element_type=jnp.float32)
        return running + product, None

    field, _ = lax.scan(add_term, jnp.zeros((TIMES, N), jnp.float32), jnp.arange(LAGS, dtype=jnp.int32))
    return excitation - field
```

```python
import functools

import jax
import jax.numpy as jnp
from jax import lax
from jax.experimental import pallas as pl
from jax.experimental.pallas import tpu as pltpu
from jax.sharding import PartitionSpec as P

MESH = pl.DeviceIdType.MESH
PAD = 16
PIECES = 2


def kernel(planes, cur_ref, pan_ref, exc_ref, out_ref, buf, pan, exc, acc, give, got, over, landed,
           send_sem, own_sem, sib_sem, half_sem, load_sem, give_sem, over_sem):
    lag, row = lax.axis_index("lag"), lax.axis_index("row")
    x, c = lag // 2, lag % 2
    z, y = row // 2, row % 2
    nx, ny = 1 - x, 1 - y
    steps, width = cur_ref.shape
    rows = 2 * planes
    half = steps // 2
    to_x, to_y = (2 * nx + c, row), (lag, 2 * z + ny)
    to_s = (2 * x + 1 - c, row)
    to_up, to_down = (lag, row + 2), (lag, row - 2)
    has_up, has_down = z + 1 < planes, z >= 1

    barrier = pltpu.get_barrier_semaphore()

    def greet(device):
        pl.semaphore_signal(barrier, inc=1, device_id=device, device_id_type=MESH)

    greet(to_s)
    greet(to_x)
    greet(to_y)
    pl.when(has_up)(lambda: greet(to_up))
    pl.when(has_down)(lambda: greet(to_down))

    loads = [pltpu.make_async_copy(cur_ref, buf.at[row, lag], load_sem.at[0]),
             pltpu.make_async_copy(exc_ref, exc, load_sem.at[1])]
    for r in range(rows):
        loads.append(pltpu.make_async_copy(
            pan_ref.at[0, :, pl.ds(r * width, width)], pan.at[r], load_sem.at[2 + r]))
    for load in loads:
        load.start()

    pl.semaphore_wait(barrier, 3 + has_up.astype(jnp.int32) + has_down.astype(jnp.int32))

    sent = []

    def send(src, dst, sem, device, guards=()):
        slot = len(sent)

        def make():
            return pltpu.make_async_remote_copy(
                src_ref=src(), dst_ref=dst(), send_sem=send_sem.at[slot], recv_sem=sem(),
                device_id=device, device_id_type=MESH)

        sent.append((guards, make))
        make().start()

    def place(bx, by, bz):
        return lambda: buf.at[2 * bz + by, 2 * bx + c]

    def mark(sems, bx, by, bz):
        return lambda: sems.at[(2 * bz + by) * 2 + bx]

    def arrive(dst, sem):
        pltpu.make_async_remote_copy(
            src_ref=dst, dst_ref=dst, send_sem=send_sem.at[0], recv_sem=sem,
            device_id=to_s, device_id_type=MESH).wait_recv()

    def forward(bx, by, bz, device, guards=(), src=None):
        send(src or place(bx, by, bz), place(bx, by, bz), mark(own_sem, bx, by, bz), device, guards)

    def share(bx, by, bz, guards=(), src=None):
        send(src or place(bx, by, bz), place(bx, by, bz), mark(sib_sem, bx, by, bz), to_s, guards)

    def take(bx, by, bz):
        arrive(place(bx, by, bz)(), mark(own_sem, bx, by, bz)())

    def part(bx, by, bz, h):
        return lambda: buf.at[2 * bz + by, 2 * bx + c, pl.ds(h * half, half)]

    def when(guard, body):
        pl.when(guard)(body)

    mine = lambda: cur_ref
    forward(x, y, z, to_x, src=mine)
    forward(x, y, z, to_y, src=mine)
    when(has_up, lambda: forward(x, y, z, to_up, (has_up,), mine))
    when(has_down, lambda: forward(x, y, z, to_down, (has_down,), mine))
    share(x, y, z, src=mine)

    acc[...] = jnp.zeros_like(acc)

    def go_on(bx, by, bz, up, guard):
        g, device = (has_up, to_up) if up else (has_down, to_down)
        when(g, lambda: forward(bx, by, bz, device, (guard, g)))

    def column(up, d):
        bz = z - d if up else z + d
        guard = bz >= 0 if up else bz < planes

        def body():
            take(x, y, bz)
            if d < planes - 1:
                go_on(x, y, bz, up, guard)
            forward(x, y, bz, to_x, (guard,))
            forward(x, y, bz, to_y, (guard,))
            share(x, y, bz, (guard,))

        when(guard, body)

    def diagonal(up, d):
        bz = z - d if up else z + d
        guard = bz >= 0 if up else bz < planes

        def body():
            take(nx, ny, bz)
            if d < planes - 1:
                go_on(nx, ny, bz, up, guard)
            share(nx, ny, bz, (guard,))

        when(guard, body)

    def sides(up, d):
        bz = z - d if up else z + d
        guard = bz >= 0 if up else bz < planes

        def body():
            take(nx, y, bz)
            share(nx, y, bz, (guard,))
            take(x, ny, bz)
            share(x, ny, bz, (guard,))

        when(guard, body)

    def multiply(by, bz):
        for bx in (0, 1):
            arrive(buf.at[2 * bz + by, 2 * bx + 1 - c], mark(sib_sem, bx, by, bz)())
        r = 2 * bz + by
        lhs = buf[r].reshape(-1, width)
        acc[pl.ds(PAD, lhs.shape[0]), :] += lax.dot_general(
            lhs, pan[r], (((1,), (1,)), ((), ())), preferred_element_type=jnp.float32)

    def multiply_plane(up, d):
        bz = z - d if up else z + d
        guard = bz >= 0 if up else bz < planes

        def body():
            @pl.loop(0, 2)
            def _(by):
                multiply(by, bz)

        when(guard, body)

    take(nx, y, z)
    send(part(nx, y, z, 0), part(nx, y, z, 0), lambda: half_sem.at[0], to_y)
    share(nx, y, z)
    take(x, ny, z)
    send(part(x, ny, z, 1), part(x, ny, z, 1), lambda: half_sem.at[1], to_x)
    share(x, ny, z)
    if planes > 1:
        column(True, 1)
        column(False, 1)
    for h in (0, 1):
        arrive(part(nx, ny, z, h)(), half_sem.at[h])
    when(has_up, lambda: forward(nx, ny, z, to_up, (has_up,)))
    when(has_down, lambda: forward(nx, ny, z, to_down, (has_down,)))
    share(nx, ny, z)
    if planes > 2:
        column(True, 2)
        column(False, 2)
    if planes > 1:
        diagonal(True, 1)
        diagonal(False, 1)
    for load in loads:
        load.wait()

    @pl.loop(0, 2)
    def _(by):
        multiply(by, z)

    for d in range(1, planes):
        if d + 2 < planes:
            column(True, d + 2)
            column(False, d + 2)
        if d + 1 < planes:
            diagonal(True, d + 1)
            diagonal(False, d + 1)
        for up in (True, False):
            sides(up, d)
        for up in (True, False):
            multiply_plane(up, d)

    piece = steps // PIECES

    def shifted(bx, core, p):
        first = pl.multiple_of(PAD - 8 + (2 * bx + core) * steps + p * piece, 8)
        window = acc[pl.ds(first, piece + 8), :]
        return pltpu.roll(window, piece + lag, 0)[:piece]

    order = [(0, p) for p in range(PIECES)] + [(1, p) for p in range(PIECES)]
    for j, p in order:
        give[j, p] = shifted(nx if j == 0 else x, 1 - c, p)
        send(lambda j=j, p=p: give.at[j, p], lambda j=j, p=p: got.at[j, p],
             lambda j=j, p=p: give_sem.at[j * PIECES + p], to_s)
    for p in range(PIECES):
        arrive(got.at[0, p], give_sem.at[p])
        over[p] = shifted(nx, c, p) + got[0, p]
        send(lambda p=p: over.at[p], lambda p=p: landed.at[p], lambda p=p: over_sem.at[p], to_x)
    for p in range(PIECES):
        arrive(got.at[1, p], give_sem.at[PIECES + p])
        at = pl.ds(p * piece, piece)
        exc[at, :] = exc[at, :] - (shifted(x, c, p) + got[1, p])
    for p in range(PIECES):
        arrive(landed.at[p], over_sem.at[p])
        at = pl.ds(p * piece, piece)
        out_ref[at, :] = exc[at, :] - landed[p]

    for guards, make in sent:
        if guards:
            g = functools.reduce(jnp.logical_and, guards)
            pl.when(g)(lambda make=make: make().wait_send())
        else:
            make().wait_send()


def fused(currents, panels, excitation):
    steps, width = currents.shape
    count = panels.shape[1]
    lags, rows = lax.axis_size("lag"), lax.axis_size("row")
    planes = rows // 2
    any_spec = pl.BlockSpec(memory_space=pl.ANY)
    dma = pltpu.SemaphoreType.DMA
    piece = steps // PIECES
    return pl.pallas_call(
        functools.partial(kernel, planes),
        out_shape=jax.ShapeDtypeStruct(excitation.shape, jnp.float32),
        in_specs=[any_spec] * 3,
        out_specs=pl.BlockSpec(memory_space=pltpu.VMEM),
        scratch_shapes=[
            pltpu.VMEM((rows, lags, steps, width), jnp.bfloat16),
            pltpu.VMEM((rows, count, width), jnp.bfloat16),
            pltpu.VMEM((steps, count), jnp.float32),
            pltpu.VMEM((PAD + lags * steps, count), jnp.float32),
            pltpu.VMEM((2, PIECES, piece, count), jnp.float32),
            pltpu.VMEM((2, PIECES, piece, count), jnp.float32),
            pltpu.VMEM((PIECES, piece, count), jnp.float32),
            pltpu.VMEM((PIECES, piece, count), jnp.float32),
            dma((24 + 16 * planes + 3 * PIECES,)),
            dma((2 * rows,)),
            dma((2 * rows,)),
            dma((2,)),
            dma((2 + rows,)),
            dma((2 * PIECES,)),
            dma((PIECES,)),
        ],
        compiler_params=pltpu.CompilerParams(
            collective_id=0, has_side_effects=True, vmem_limit_bytes=40 * 2**20),
        cost_estimate=pl.CostEstimate(
            flops=2 * lags * steps * width * rows * count,
            bytes_accessed=panels.size * 2, transcendentals=0),
    )(currents, panels, excitation)


def plain(currents, panels, excitation):
    gathered = lax.all_gather(currents, "row", axis=1, tiled=True)
    block_len = currents.shape[0]
    lag_total = lax.axis_size("lag")
    lag_index = lax.axis_index("lag")
    all_times = block_len * lag_total
    running = jnp.zeros((all_times + lag_total, panels.shape[1]), jnp.float32)
    product = lax.dot_general(
        lax.all_gather(gathered, "lag", axis=0, tiled=True),
        panels[0],
        (((1,), (1,)), ((), ())),
        preferred_element_type=jnp.float32,
    )
    running = lax.dynamic_update_slice_in_dim(running, product, lag_index, 0)
    field = lax.psum_scatter(running[:all_times], "lag", scatter_dimension=0, tiled=True)
    return excitation - field


def solution(mesh):
    paired = mesh.shape["lag"] == 4 and mesh.shape["row"] % 2 == 0
    return jax.shard_map(
        fused if paired else plain,
        mesh=mesh,
        in_specs=(P("lag", "row"), P("lag", "row", None), P("lag", "row")),
        out_specs=P("lag", "row"),
        check_vma=False,
    )
```

```python
import functools

import jax
import jax.numpy as jnp
from jax import lax
from jax.experimental import pallas as pl
from jax.experimental.pallas import tpu as pltpu
from jax.sharding import PartitionSpec as P

MESH = pl.DeviceIdType.MESH
PAD = 16
PIECES = 2


def kernel(planes, cur_ref, pan_ref, exc_ref, out_ref, buf, pan, exc, acc, give, got, over, landed,
           send_sem, own_sem, sib_sem, half_sem, load_sem, give_sem, over_sem):
    lag, row = lax.axis_index("lag"), lax.axis_index("row")
    x, c = lag // 2, lag % 2
    z, y = row // 2, row % 2
    nx, ny = 1 - x, 1 - y
    steps, width = cur_ref.shape
    rows = 2 * planes
    half = steps // 2
    to_x, to_y = (2 * nx + c, row), (lag, 2 * z + ny)
    to_s = (2 * x + 1 - c, row)
    to_up, to_down = (lag, row + 2), (lag, row - 2)
    has_up, has_down = z + 1 < planes, z >= 1

    barrier = pltpu.get_barrier_semaphore()

    def greet(device):
        pl.semaphore_signal(barrier, inc=1, device_id=device, device_id_type=MESH)

    greet(to_s)
    greet(to_x)
    greet(to_y)
    pl.when(has_up)(lambda: greet(to_up))
    pl.when(has_down)(lambda: greet(to_down))

    loads = [pltpu.make_async_copy(cur_ref, buf.at[row, lag], load_sem.at[0]),
             pltpu.make_async_copy(exc_ref, exc, load_sem.at[1])]
    for r in range(rows):
        loads.append(pltpu.make_async_copy(
            pan_ref.at[0, :, pl.ds(r * width, width)], pan.at[r], load_sem.at[2 + r]))
    for load in loads:
        load.start()

    pl.semaphore_wait(barrier, 3 + has_up.astype(jnp.int32) + has_down.astype(jnp.int32))

    sent = []

    def send(src, dst, sem, device, guards=()):
        slot = len(sent)

        def make():
            return pltpu.make_async_remote_copy(
                src_ref=src(), dst_ref=dst(), send_sem=send_sem.at[slot], recv_sem=sem(),
                device_id=device, device_id_type=MESH)

        sent.append((guards, make))
        make().start()

    def place(bx, by, bz):
        return lambda: buf.at[2 * bz + by, 2 * bx + c]

    def mark(sems, bx, by, bz):
        return lambda: sems.at[(2 * bz + by) * 2 + bx]

    def arrive(dst, sem):
        pltpu.make_async_remote_copy(
            src_ref=dst, dst_ref=dst, send_sem=send_sem.at[0], recv_sem=sem,
            device_id=to_s, device_id_type=MESH).wait_recv()

    def forward(bx, by, bz, device, guards=(), src=None):
        send(src or place(bx, by, bz), place(bx, by, bz), mark(own_sem, bx, by, bz), device, guards)

    def share(bx, by, bz, guards=(), src=None):
        send(src or place(bx, by, bz), place(bx, by, bz), mark(sib_sem, bx, by, bz), to_s, guards)

    def take(bx, by, bz):
        arrive(place(bx, by, bz)(), mark(own_sem, bx, by, bz)())

    def part(bx, by, bz, h):
        return lambda: buf.at[2 * bz + by, 2 * bx + c, pl.ds(h * half, half)]

    def when(guard, body):
        pl.when(guard)(body)

    mine = lambda: cur_ref
    forward(x, y, z, to_x, src=mine)
    forward(x, y, z, to_y, src=mine)
    when(has_up, lambda: forward(x, y, z, to_up, (has_up,), mine))
    when(has_down, lambda: forward(x, y, z, to_down, (has_down,), mine))
    share(x, y, z, src=mine)

    acc[...] = jnp.zeros_like(acc)

    def go_on(bx, by, bz, up, guard):
        g, device = (has_up, to_up) if up else (has_down, to_down)
        when(g, lambda: forward(bx, by, bz, device, (guard, g)))

    def column(up, d):
        bz = z - d if up else z + d
        guard = bz >= 0 if up else bz < planes

        def body():
            take(x, y, bz)
            if d < planes - 1:
                go_on(x, y, bz, up, guard)
            forward(x, y, bz, to_x, (guard,))
            forward(x, y, bz, to_y, (guard,))
            share(x, y, bz, (guard,))

        when(guard, body)

    last = planes - 1 if planes >= 3 else planes

    def diagonal(up, d):
        bz = z - d if up else z + d
        guard = bz >= 0 if up else bz < planes

        def body():
            if d < last:
                take(nx, ny, bz)
                if d + 1 < last:
                    go_on(nx, ny, bz, up, guard)
            else:
                for h in (0, 1):
                    arrive(part(nx, ny, bz, h)(), half_sem.at[2 + h])
            share(nx, ny, bz, (guard,))

        when(guard, body)

    def sides(up, d):
        bz = z - d if up else z + d
        guard = bz >= 0 if up else bz < planes

        def body():
            take(nx, y, bz)
            if d == last:
                send(part(nx, y, bz, 0), part(nx, y, bz, 0), lambda: half_sem.at[2], to_y, (guard,))
            share(nx, y, bz, (guard,))
            take(x, ny, bz)
            if d == last:
                send(part(x, ny, bz, 1), part(x, ny, bz, 1), lambda: half_sem.at[3], to_x, (guard,))
            share(x, ny, bz, (guard,))

        when(guard, body)

    def multiply(by, bz):
        for bx in (0, 1):
            arrive(buf.at[2 * bz + by, 2 * bx + 1 - c], mark(sib_sem, bx, by, bz)())
        r = 2 * bz + by
        lhs = buf[r].reshape(-1, width)
        acc[pl.ds(PAD, lhs.shape[0]), :] += lax.dot_general(
            lhs, pan[r], (((1,), (1,)), ((), ())), preferred_element_type=jnp.float32)

    def multiply_plane(up, d):
        bz = z - d if up else z + d
        guard = bz >= 0 if up else bz < planes

        def body():
            @pl.loop(0, 2)
            def _(by):
                multiply(by, bz)

        when(guard, body)

    take(nx, y, z)
    send(part(nx, y, z, 0), part(nx, y, z, 0), lambda: half_sem.at[0], to_y)
    share(nx, y, z)
    take(x, ny, z)
    send(part(x, ny, z, 1), part(x, ny, z, 1), lambda: half_sem.at[1], to_x)
    share(x, ny, z)
    if planes > 1:
        column(True, 1)
        column(False, 1)
    for h in (0, 1):
        arrive(part(nx, ny, z, h)(), half_sem.at[h])
    when(has_up, lambda: forward(nx, ny, z, to_up, (has_up,)))
    when(has_down, lambda: forward(nx, ny, z, to_down, (has_down,)))
    share(nx, ny, z)
    def both(step, d):
        if 1 <= d < planes:
            step(True, d)
            step(False, d)

    both(column, 2)
    if last > 1:
        both(diagonal, 1)
    for load in loads:
        load.wait()

    @pl.loop(0, 2)
    def _(by):
        multiply(by, z)

    both(column, 3)
    if last > 2:
        both(diagonal, 2)
    both(sides, 1)
    if last > 1:
        both(multiply_plane, 1)
    for d in range(2, planes):
        if d + 2 < planes:
            both(column, d + 2)
        if d + 1 < last:
            both(diagonal, d + 1)
        both(sides, d)
        if d == last:
            if d > 2:
                both(multiply_plane, d - 1)
            both(diagonal, d)
            both(multiply_plane, d)
        elif d + 1 < last:
            both(multiply_plane, d)
    piece = steps // PIECES

    def shifted(bx, core, p):
        first = pl.multiple_of(PAD - 8 + (2 * bx + core) * steps + p * piece, 8)
        window = acc[pl.ds(first, piece + 8), :]
        return pltpu.roll(window, piece + lag, 0)[:piece]

    order = [(0, p) for p in range(PIECES)] + [(1, p) for p in range(PIECES)]
    for j, p in order:
        give[j, p] = shifted(nx if j == 0 else x, 1 - c, p)
        send(lambda j=j, p=p: give.at[j, p], lambda j=j, p=p: got.at[j, p],
             lambda j=j, p=p: give_sem.at[j * PIECES + p], to_s)
    for p in range(PIECES):
        arrive(got.at[0, p], give_sem.at[p])
        over[p] = shifted(nx, c, p) + got[0, p]
        send(lambda p=p: over.at[p], lambda p=p: landed.at[p], lambda p=p: over_sem.at[p], to_x)
    for p in range(PIECES):
        arrive(got.at[1, p], give_sem.at[PIECES + p])
        at = pl.ds(p * piece, piece)
        exc[at, :] = exc[at, :] - (shifted(x, c, p) + got[1, p])
    for p in range(PIECES):
        arrive(landed.at[p], over_sem.at[p])
        at = pl.ds(p * piece, piece)
        out_ref[at, :] = exc[at, :] - landed[p]

    for guards, make in sent:
        if guards:
            g = functools.reduce(jnp.logical_and, guards)
            pl.when(g)(lambda make=make: make().wait_send())
        else:
            make().wait_send()


def fused(currents, panels, excitation):
    steps, width = currents.shape
    count = panels.shape[1]
    lags, rows = lax.axis_size("lag"), lax.axis_size("row")
    planes = rows // 2
    hbm_spec = pl.BlockSpec(memory_space=pltpu.HBM)
    dma = pltpu.SemaphoreType.DMA
    piece = steps // PIECES
    return pl.pallas_call(
        functools.partial(kernel, planes),
        out_shape=jax.ShapeDtypeStruct(excitation.shape, jnp.float32),
        in_specs=[hbm_spec] * 3,
        out_specs=pl.BlockSpec(memory_space=pltpu.VMEM),
        scratch_shapes=[
            pltpu.VMEM((rows, lags, steps, width), jnp.bfloat16),
            pltpu.VMEM((rows, count, width), jnp.bfloat16),
            pltpu.VMEM((steps, count), jnp.float32),
            pltpu.VMEM((PAD + lags * steps, count), jnp.float32),
            pltpu.VMEM((2, PIECES, piece, count), jnp.float32),
            pltpu.VMEM((2, PIECES, piece, count), jnp.float32),
            pltpu.VMEM((PIECES, piece, count), jnp.float32),
            pltpu.VMEM((PIECES, piece, count), jnp.float32),
            dma((24 + 20 * planes + 3 * PIECES,)),
            dma((2 * rows,)),
            dma((2 * rows,)),
            dma((4,)),
            dma((2 + rows,)),
            dma((2 * PIECES,)),
            dma((PIECES,)),
        ],
        compiler_params=pltpu.CompilerParams(
            collective_id=0, has_side_effects=True, vmem_limit_bytes=64 * 2**20),
        cost_estimate=pl.CostEstimate(
            flops=2 * lags * steps * width * rows * count,
            bytes_accessed=panels.size * 2, transcendentals=0),
    )(currents, panels, excitation)


def plain(currents, panels, excitation):
    gathered = lax.all_gather(currents, "row", axis=1, tiled=True)
    block_len = currents.shape[0]
    lag_total = lax.axis_size("lag")
    lag_index = lax.axis_index("lag")
    all_times = block_len * lag_total
    running = jnp.zeros((all_times + lag_total, panels.shape[1]), jnp.float32)
    product = lax.dot_general(
        lax.all_gather(gathered, "lag", axis=0, tiled=True),
        panels[0],
        (((1,), (1,)), ((), ())),
        preferred_element_type=jnp.float32,
    )
    running = lax.dynamic_update_slice_in_dim(running, product, lag_index, 0)
    field = lax.psum_scatter(running[:all_times], "lag", scatter_dimension=0, tiled=True)
    return excitation - field


def solution(mesh):
    paired = mesh.shape["lag"] == 4 and mesh.shape["row"] % 2 == 0
    return jax.shard_map(
        fused if paired else plain,
        mesh=mesh,
        in_specs=(P("lag", "row"), P("lag", "row", None), P("lag", "row")),
        out_specs=P("lag", "row"),
        check_vma=False,
    )
```

```python
import functools

import jax
import jax.numpy as jnp
from jax import lax
from jax.experimental import pallas as pl
from jax.experimental.pallas import tpu as pltpu
from jax.sharding import PartitionSpec as P

MESH = pl.DeviceIdType.MESH
PAD = 16
PIECES = 4
HALVES = (0, 1)


def kernel(planes, cur_ref, pan_ref, exc_ref, out_ref, buf, pan, exc, acc, give, got, over, landed,
           send_sem, own_sem, sib_sem, load_sem, give_sem, over_sem):
    lag, row = lax.axis_index("lag"), lax.axis_index("row")
    x, c = lag // 2, lag % 2
    z, y = row // 2, row % 2
    nx, ny = 1 - x, 1 - y
    steps, width = cur_ref.shape
    rows = 2 * planes
    half = steps // 2
    to_x, to_y = (2 * nx + c, row), (lag, 2 * z + ny)
    to_s = (2 * x + 1 - c, row)
    to_up, to_down = (lag, row + 2), (lag, row - 2)
    has_up, has_down = z + 1 < planes, z >= 1

    barrier = pltpu.get_barrier_semaphore()

    def greet(device):
        pl.semaphore_signal(barrier, inc=1, device_id=device, device_id_type=MESH)

    greet(to_s)
    greet(to_x)
    greet(to_y)
    pl.when(has_up)(lambda: greet(to_up))
    pl.when(has_down)(lambda: greet(to_down))

    loads = [pltpu.make_async_copy(cur_ref, buf.at[row, lag], load_sem.at[0]),
             pltpu.make_async_copy(exc_ref, exc, load_sem.at[1])]
    for r in range(rows):
        loads.append(pltpu.make_async_copy(
            pan_ref.at[0, :, pl.ds(r * width, width)], pan.at[r], load_sem.at[2 + r]))
    for load in loads:
        load.start()

    pl.semaphore_wait(barrier, 3 + has_up.astype(jnp.int32) + has_down.astype(jnp.int32))

    sent = []

    def send(src, dst, sem, device, guards=()):
        slot = len(sent)

        def make():
            return pltpu.make_async_remote_copy(
                src_ref=src(), dst_ref=dst(), send_sem=send_sem.at[slot], recv_sem=sem(),
                device_id=device, device_id_type=MESH)

        sent.append((guards, make))
        make().start()

    def place(bx, by, bz):
        return lambda: buf.at[2 * bz + by, 2 * bx + c]

    def part(bx, by, bz, h):
        return lambda: buf.at[2 * bz + by, 2 * bx + c, pl.ds(h * half, half)]

    def part_mark(bx, by, bz, h):
        return lambda: own_sem.at[((2 * bz + by) * 2 + bx) * 2 + h]

    def share_mark(bx, by, bz):
        return lambda: sib_sem.at[(2 * bz + by) * 2 + bx]

    def arrive(dst, sem):
        pltpu.make_async_remote_copy(
            src_ref=dst, dst_ref=dst, send_sem=send_sem.at[0], recv_sem=sem,
            device_id=to_s, device_id_type=MESH).wait_recv()

    def forward(bx, by, bz, h, device, guards=(), src=None):
        send(src or part(bx, by, bz, h), part(bx, by, bz, h), part_mark(bx, by, bz, h), device, guards)

    def share(bx, by, bz, guards=(), src=None):
        send(src or place(bx, by, bz), place(bx, by, bz), share_mark(bx, by, bz), to_s, guards)

    def take(bx, by, bz, h):
        arrive(part(bx, by, bz, h)(), part_mark(bx, by, bz, h)())

    def when(guard, body):
        pl.when(guard)(body)

    for h in HALVES:
        mine = lambda h=h: cur_ref.at[pl.ds(h * half, half)]
        when(has_up, lambda: forward(x, y, z, h, to_up, (has_up,), mine))
        when(has_down, lambda: forward(x, y, z, h, to_down, (has_down,), mine))
        forward(x, y, z, h, to_x, src=mine)
        forward(x, y, z, h, to_y, src=mine)
    share(x, y, z, src=lambda: cur_ref)

    acc[...] = jnp.zeros_like(acc)

    def go_on(bx, by, bz, h, up, guard):
        g, device = (has_up, to_up) if up else (has_down, to_down)
        when(g, lambda: forward(bx, by, bz, h, device, (guard, g)))

    def at_plane(up, d):
        return (z - d, z >= d) if up else (z + d, z + d < planes)

    def column(up, d, h):
        bz, guard = at_plane(up, d)

        def body():
            take(x, y, bz, h)
            if d < planes - 1:
                go_on(x, y, bz, h, up, guard)
            forward(x, y, bz, h, to_x, (guard,))
            forward(x, y, bz, h, to_y, (guard,))
            if h == 1:
                share(x, y, bz, (guard,))

        when(guard, body)

    last = planes - 1 if planes >= 3 else planes

    def diagonal(up, d, h):
        bz, guard = at_plane(up, d)

        def body():
            take(nx, ny, bz, h)
            if d + 1 < last:
                go_on(nx, ny, bz, h, up, guard)
            if h == 1:
                share(nx, ny, bz, (guard,))

        when(guard, body)

    def side(bz, guards, turn):
        take(nx, y, bz, 0)
        if turn:
            forward(nx, y, bz, 0, to_y, guards)
        take(x, ny, bz, 0)
        take(x, ny, bz, 1)
        if turn:
            forward(x, ny, bz, 1, to_x, guards)
        take(nx, y, bz, 1)
        share(nx, y, bz, guards)
        share(x, ny, bz, guards)

    def sides(up, d, h):
        bz, guard = at_plane(up, d)
        if h == 0:
            when(guard, lambda: side(bz, (guard,), d == last))

    def multiply(by, bz):
        for bx in (0, 1):
            arrive(buf.at[2 * bz + by, 2 * bx + 1 - c], share_mark(bx, by, bz)())
        r = 2 * bz + by
        lhs = buf[r].reshape(-1, width)
        acc[pl.ds(PAD, lhs.shape[0]), :] += lax.dot_general(
            lhs, pan[r], (((1,), (1,)), ((), ())), preferred_element_type=jnp.float32)

    def multiply_plane(up, d, h):
        bz, guard = at_plane(up, d)
        if h == 1:
            return

        def body():
            @pl.loop(0, 2)
            def _(by):
                multiply(by, bz)

        when(guard, body)

    def both(step, d):
        if 1 <= d < planes:
            for h in HALVES:
                step(True, d, h)
                step(False, d, h)

    side(z, (), True)
    both(column, 1)
    for h in HALVES:
        take(nx, ny, z, h)
        when(has_up, lambda: forward(nx, ny, z, h, to_up, (has_up,)))
        when(has_down, lambda: forward(nx, ny, z, h, to_down, (has_down,)))
    share(nx, ny, z)
    both(column, 2)
    if last > 1:
        both(diagonal, 1)
    for load in loads:
        load.wait()

    @pl.loop(0, 2)
    def _(by):
        multiply(by, z)

    both(column, 3)
    if last > 2:
        both(diagonal, 2)
    both(sides, 1)
    if last > 1:
        both(multiply_plane, 1)
    for d in range(2, planes):
        if d + 2 < planes:
            both(column, d + 2)
        if d + 1 < last:
            both(diagonal, d + 1)
        both(sides, d)
        if d == last:
            if d > 2:
                both(multiply_plane, d - 1)
            both(diagonal, d)
            both(multiply_plane, d)
        elif d + 1 < last:
            both(multiply_plane, d)
    piece = steps // PIECES

    def shifted(bx, core, p):
        first = pl.multiple_of(PAD - 8 + (2 * bx + core) * steps + p * piece, 8)
        window = acc[pl.ds(first, piece + 8), :]
        return pltpu.roll(window, piece + lag, 0)[:piece]

    order = [(0, p) for p in range(PIECES)] + [(1, p) for p in range(PIECES)]
    for j, p in order:
        give[j, p] = shifted(nx if j == 0 else x, 1 - c, p)
        send(lambda j=j, p=p: give.at[j, p], lambda j=j, p=p: got.at[j, p],
             lambda j=j, p=p: give_sem.at[j * PIECES + p], to_s)
    for p in range(PIECES):
        arrive(got.at[0, p], give_sem.at[p])
        over[p] = shifted(nx, c, p) + got[0, p]
        send(lambda p=p: over.at[p], lambda p=p: landed.at[p], lambda p=p: over_sem.at[p], to_x)
    for p in range(PIECES):
        arrive(got.at[1, p], give_sem.at[PIECES + p])
        at = pl.ds(p * piece, piece)
        exc[at, :] = exc[at, :] - (shifted(x, c, p) + got[1, p])
    for p in range(PIECES):
        arrive(landed.at[p], over_sem.at[p])
        at = pl.ds(p * piece, piece)
        out_ref[at, :] = exc[at, :] - landed[p]

    for guards, make in sent:
        if guards:
            g = functools.reduce(jnp.logical_and, guards)
            pl.when(g)(lambda make=make: make().wait_send())
        else:
            make().wait_send()


def fused(currents, panels, excitation):
    steps, width = currents.shape
    count = panels.shape[1]
    lags, rows = lax.axis_size("lag"), lax.axis_size("row")
    planes = rows // 2
    hbm_spec = pl.BlockSpec(memory_space=pltpu.HBM)
    dma = pltpu.SemaphoreType.DMA
    piece = steps // PIECES
    return pl.pallas_call(
        functools.partial(kernel, planes),
        out_shape=jax.ShapeDtypeStruct(excitation.shape, jnp.float32),
        in_specs=[hbm_spec] * 3,
        out_specs=pl.BlockSpec(memory_space=pltpu.VMEM),
        scratch_shapes=[
            pltpu.VMEM((rows, lags, steps, width), jnp.bfloat16),
            pltpu.VMEM((rows, count, width), jnp.bfloat16),
            pltpu.VMEM((steps, count), jnp.float32),
            pltpu.VMEM((PAD + lags * steps, count), jnp.float32),
            pltpu.VMEM((2, PIECES, piece, count), jnp.float32),
            pltpu.VMEM((2, PIECES, piece, count), jnp.float32),
            pltpu.VMEM((PIECES, piece, count), jnp.float32),
            pltpu.VMEM((PIECES, piece, count), jnp.float32),
            dma((24 + 32 * planes + 3 * PIECES,)),
            dma((4 * rows,)),
            dma((2 * rows,)),
            dma((2 + rows,)),
            dma((2 * PIECES,)),
            dma((PIECES,)),
        ],
        compiler_params=pltpu.CompilerParams(
            collective_id=0, has_side_effects=True, vmem_limit_bytes=64 * 2**20),
        cost_estimate=pl.CostEstimate(
            flops=2 * lags * steps * width * rows * count,
            bytes_accessed=panels.size * 2, transcendentals=0),
    )(currents, panels, excitation)


def plain(currents, panels, excitation):
    gathered = lax.all_gather(currents, "row", axis=1, tiled=True)
    block_len = currents.shape[0]
    lag_total = lax.axis_size("lag")
    lag_index = lax.axis_index("lag")
    all_times = block_len * lag_total
    running = jnp.zeros((all_times + lag_total, panels.shape[1]), jnp.float32)
    product = lax.dot_general(
        lax.all_gather(gathered, "lag", axis=0, tiled=True),
        panels[0],
        (((1,), (1,)), ((), ())),
        preferred_element_type=jnp.float32,
    )
    running = lax.dynamic_update_slice_in_dim(running, product, lag_index, 0)
    field = lax.psum_scatter(running[:all_times], "lag", scatter_dimension=0, tiled=True)
    return excitation - field


def solution(mesh):
    paired = mesh.shape["lag"] == 4 and mesh.shape["row"] % 2 == 0
    return jax.shard_map(
        fused if paired else plain,
        mesh=mesh,
        in_specs=(P("lag", "row"), P("lag", "row", None), P("lag", "row")),
        out_specs=P("lag", "row"),
        check_vma=False,
    )
```

```python
import functools

import jax
import jax.numpy as jnp
from jax import lax
from jax.experimental import pallas as pl
from jax.experimental.pallas import tpu as pltpu
from jax.sharding import PartitionSpec as P

MESH = pl.DeviceIdType.MESH
PAD = 16
PIECES = 4
HALVES = (0, 1)


def kernel(planes, cur_ref, pan_ref, exc_ref, out_ref, buf, pan, exc, acc, give, got, over, landed,
           send_sem, own_sem, sib_sem, load_sem, give_sem, over_sem):
    lag, row = lax.axis_index("lag"), lax.axis_index("row")
    x, c = lag // 2, lag % 2
    z, y = row // 2, row % 2
    nx, ny = 1 - x, 1 - y
    steps, width = cur_ref.shape
    rows = 2 * planes
    half = steps // 2
    to_x, to_y = (2 * nx + c, row), (lag, 2 * z + ny)
    to_s = (2 * x + 1 - c, row)
    to_up, to_down = (lag, row + 2), (lag, row - 2)
    has_up, has_down = z + 1 < planes, z >= 1

    barrier = pltpu.get_barrier_semaphore()

    def greet(device):
        pl.semaphore_signal(barrier, inc=1, device_id=device, device_id_type=MESH)

    greet(to_s)
    greet(to_x)
    greet(to_y)
    pl.when(has_up)(lambda: greet(to_up))
    pl.when(has_down)(lambda: greet(to_down))

    loads = [pltpu.make_async_copy(cur_ref, buf.at[row, lag], load_sem.at[0]),
             pltpu.make_async_copy(exc_ref, exc, load_sem.at[1])]
    for r in range(rows):
        loads.append(pltpu.make_async_copy(
            pan_ref.at[0, :, pl.ds(r * width, width)], pan.at[r], load_sem.at[2 + r]))
    for load in loads:
        load.start()

    pl.semaphore_wait(barrier, 3 + has_up.astype(jnp.int32) + has_down.astype(jnp.int32))

    sent = []

    def send(src, dst, sem, device, guards=()):
        slot = len(sent)

        def make():
            return pltpu.make_async_remote_copy(
                src_ref=src(), dst_ref=dst(), send_sem=send_sem.at[slot], recv_sem=sem(),
                device_id=device, device_id_type=MESH)

        sent.append((guards, make))
        make().start()

    def place(bx, by, bz):
        return lambda: buf.at[2 * bz + by, 2 * bx + c]

    def part(bx, by, bz, h):
        return lambda: buf.at[2 * bz + by, 2 * bx + c, pl.ds(h * half, half)]

    def part_mark(bx, by, bz, h):
        return lambda: own_sem.at[((2 * bz + by) * 2 + bx) * 2 + h]

    def share_mark(bx, by, bz):
        return lambda: sib_sem.at[(2 * bz + by) * 2 + bx]

    def arrive(dst, sem):
        pltpu.make_async_remote_copy(
            src_ref=dst, dst_ref=dst, send_sem=send_sem.at[0], recv_sem=sem,
            device_id=to_s, device_id_type=MESH).wait_recv()

    def forward(bx, by, bz, h, device, guards=(), src=None):
        send(src or part(bx, by, bz, h), part(bx, by, bz, h), part_mark(bx, by, bz, h), device, guards)

    def share(bx, by, bz, guards=(), src=None):
        send(src or place(bx, by, bz), place(bx, by, bz), share_mark(bx, by, bz), to_s, guards)

    def take(bx, by, bz, h):
        arrive(part(bx, by, bz, h)(), part_mark(bx, by, bz, h)())

    def when(guard, body):
        pl.when(guard)(body)

    for h in HALVES:
        mine = lambda h=h: cur_ref.at[pl.ds(h * half, half)]
        when(has_up, lambda: forward(x, y, z, h, to_up, (has_up,), mine))
        when(has_down, lambda: forward(x, y, z, h, to_down, (has_down,), mine))
        forward(x, y, z, h, to_x, src=mine)
        forward(x, y, z, h, to_y, src=mine)
    share(x, y, z, src=lambda: cur_ref)

    acc[...] = jnp.zeros_like(acc)

    def go_on(bx, by, bz, h, up, guard):
        g, device = (has_up, to_up) if up else (has_down, to_down)
        when(g, lambda: forward(bx, by, bz, h, device, (guard, g)))

    def at_plane(up, d):
        return (z - d, z >= d) if up else (z + d, z + d < planes)

    def column(up, d, h):
        bz, guard = at_plane(up, d)

        def body():
            take(x, y, bz, h)
            if d < planes - 1:
                go_on(x, y, bz, h, up, guard)
            forward(x, y, bz, h, to_x, (guard,))
            forward(x, y, bz, h, to_y, (guard,))
            if h == 1:
                share(x, y, bz, (guard,))

        when(guard, body)

    last = planes - 1 if planes >= 3 else planes

    def diagonal(up, d, h):
        bz, guard = at_plane(up, d)

        def body():
            take(nx, ny, bz, h)
            if d + 1 < last:
                go_on(nx, ny, bz, h, up, guard)
            if h == 1:
                share(nx, ny, bz, (guard,))

        when(guard, body)

    def side(bz, guards, turn):
        take(nx, y, bz, 0)
        if turn:
            forward(nx, y, bz, 0, to_y, guards)
        take(x, ny, bz, 0)
        take(x, ny, bz, 1)
        if turn:
            forward(x, ny, bz, 1, to_x, guards)
        take(nx, y, bz, 1)
        share(nx, y, bz, guards)
        share(x, ny, bz, guards)

    def sides(up, d, h):
        bz, guard = at_plane(up, d)
        if h == 0:
            when(guard, lambda: side(bz, (guard,), d == last))

    def multiply(by, bz):
        for bx in (0, 1):
            arrive(buf.at[2 * bz + by, 2 * bx + 1 - c], share_mark(bx, by, bz)())
        r = 2 * bz + by
        lhs = buf[r].reshape(-1, width)
        acc[pl.ds(PAD, lhs.shape[0]), :] += lax.dot_general(
            lhs, pan[r], (((1,), (1,)), ((), ())), preferred_element_type=jnp.float32)

    def multiply_near(up, d, h):
        bz, guard = at_plane(up, d)
        if h == 0:
            when(guard, lambda: multiply(y, bz))

    def multiply_far(up, d, h):
        bz, guard = at_plane(up, d)
        if h == 0:
            when(guard, lambda: multiply(ny, bz))

    def both(step, d):
        if 1 <= d < planes:
            for h in HALVES:
                step(True, d, h)
                step(False, d, h)

    side(z, (), True)
    both(column, 1)
    both(column, 2)
    for h in HALVES:
        take(nx, ny, z, h)
        when(has_up, lambda: forward(nx, ny, z, h, to_up, (has_up,)))
        when(has_down, lambda: forward(nx, ny, z, h, to_down, (has_down,)))
    share(nx, ny, z)
    if last > 1:
        both(diagonal, 1)
    for load in loads:
        load.wait()
    multiply(y, z)
    both(column, 3)
    multiply(ny, z)
    both(sides, 1)
    both(multiply_near, 1)
    if last > 2:
        both(diagonal, 2)
    if last > 1:
        both(multiply_far, 1)
    for d in range(2, planes):
        if d + 2 < planes:
            both(column, d + 2)
        if 2 < d + 1 < last:
            both(diagonal, d + 1)
        if d < last or d == 2:
            both(sides, d)
        if d < last:
            if d + 1 == last:
                both(sides, d + 1)
            both(multiply_near, d)
            both(multiply_far, d)
        else:
            both(multiply_near, d)
            both(diagonal, d)
            both(multiply_far, d)

    piece = steps // PIECES

    def shifted(bx, core, p):
        first = pl.multiple_of(PAD - 8 + (2 * bx + core) * steps + p * piece, 8)
        window = acc[pl.ds(first, piece + 8), :]
        return pltpu.roll(window, piece + lag, 0)[:piece]

    def give_piece(j, p):
        give[j, p] = shifted(nx if j == 0 else x, 1 - c, p)
        send(lambda j=j, p=p: give.at[j, p], lambda j=j, p=p: got.at[j, p],
             lambda j=j, p=p: give_sem.at[j * PIECES + p], to_s)

    for p in range(PIECES):
        give_piece(0, p)
    for p in range(PIECES):
        arrive(got.at[0, p], give_sem.at[p])
        over[p] = shifted(nx, c, p) + got[0, p]
        send(lambda p=p: over.at[p], lambda p=p: landed.at[p], lambda p=p: over_sem.at[p], to_x)
    for p in range(PIECES):
        give_piece(1, p)
    for p in range(PIECES):
        arrive(got.at[1, p], give_sem.at[PIECES + p])
        at = pl.ds(p * piece, piece)
        exc[at, :] = exc[at, :] - (shifted(x, c, p) + got[1, p])
    for p in range(PIECES):
        arrive(landed.at[p], over_sem.at[p])
        at = pl.ds(p * piece, piece)
        out_ref[at, :] = exc[at, :] - landed[p]

    for guards, make in sent:
        if guards:
            g = functools.reduce(jnp.logical_and, guards)
            pl.when(g)(lambda make=make: make().wait_send())
        else:
            make().wait_send()


def fused(currents, panels, excitation):
    steps, width = currents.shape
    count = panels.shape[1]
    lags, rows = lax.axis_size("lag"), lax.axis_size("row")
    planes = rows // 2
    hbm_spec = pl.BlockSpec(memory_space=pltpu.HBM)
    dma = pltpu.SemaphoreType.DMA
    piece = steps // PIECES
    return pl.pallas_call(
        functools.partial(kernel, planes),
        out_shape=jax.ShapeDtypeStruct(excitation.shape, jnp.float32),
        in_specs=[hbm_spec] * 3,
        out_specs=pl.BlockSpec(memory_space=pltpu.VMEM),
        scratch_shapes=[
            pltpu.VMEM((rows, lags, steps, width), jnp.bfloat16),
            pltpu.VMEM((rows, count, width), jnp.bfloat16),
            pltpu.VMEM((steps, count), jnp.float32),
            pltpu.VMEM((PAD + lags * steps, count), jnp.float32),
            pltpu.VMEM((2, PIECES, piece, count), jnp.float32),
            pltpu.VMEM((2, PIECES, piece, count), jnp.float32),
            pltpu.VMEM((PIECES, piece, count), jnp.float32),
            pltpu.VMEM((PIECES, piece, count), jnp.float32),
            dma((24 + 32 * planes + 3 * PIECES,)),
            dma((4 * rows,)),
            dma((2 * rows,)),
            dma((2 + rows,)),
            dma((2 * PIECES,)),
            dma((PIECES,)),
        ],
        compiler_params=pltpu.CompilerParams(
            collective_id=0, has_side_effects=True, vmem_limit_bytes=64 * 2**20),
        cost_estimate=pl.CostEstimate(
            flops=2 * lags * steps * width * rows * count,
            bytes_accessed=panels.size * 2, transcendentals=0),
    )(currents, panels, excitation)


def plain(currents, panels, excitation):
    gathered = lax.all_gather(currents, "row", axis=1, tiled=True)
    block_len = currents.shape[0]
    lag_total = lax.axis_size("lag")
    lag_index = lax.axis_index("lag")
    all_times = block_len * lag_total
    running = jnp.zeros((all_times + lag_total, panels.shape[1]), jnp.float32)
    product = lax.dot_general(
        lax.all_gather(gathered, "lag", axis=0, tiled=True),
        panels[0],
        (((1,), (1,)), ((), ())),
        preferred_element_type=jnp.float32,
    )
    running = lax.dynamic_update_slice_in_dim(running, product, lag_index, 0)
    field = lax.psum_scatter(running[:all_times], "lag", scatter_dimension=0, tiled=True)
    return excitation - field


def solution(mesh):
    paired = mesh.shape["lag"] == 4 and mesh.shape["row"] % 2 == 0
    return jax.shard_map(
        fused if paired else plain,
        mesh=mesh,
        in_specs=(P("lag", "row"), P("lag", "row", None), P("lag", "row")),
        out_specs=P("lag", "row"),
        check_vma=False,
    )
```

```python
import functools

import jax
import jax.numpy as jnp
from jax import lax
from jax.experimental import pallas as pl
from jax.experimental.pallas import tpu as pltpu
from jax.sharding import PartitionSpec as P

MESH = pl.DeviceIdType.MESH
PAD = 16
PIECES = 4
HALVES = (0, 1)


def kernel(planes, cur_ref, pan_ref, exc_ref, out_ref, buf, pan, exc, acc, give, got, over, landed,
           send_sem, own_sem, sib_sem, load_sem, give_sem, over_sem):
    lag, row = lax.axis_index("lag"), lax.axis_index("row")
    x, c = lag // 2, lag % 2
    z, y = row // 2, row % 2
    nx, ny = 1 - x, 1 - y
    steps, width = cur_ref.shape
    rows = 2 * planes
    half = steps // 2
    to_x, to_y = (2 * nx + c, row), (lag, 2 * z + ny)
    to_s = (2 * x + 1 - c, row)
    to_up, to_down = (lag, row + 2), (lag, row - 2)
    has_up, has_down = z + 1 < planes, z >= 1

    barrier = pltpu.get_barrier_semaphore()

    def greet(device):
        pl.semaphore_signal(barrier, inc=1, device_id=device, device_id_type=MESH)

    greet(to_s)
    greet(to_x)
    greet(to_y)
    pl.when(has_up)(lambda: greet(to_up))
    pl.when(has_down)(lambda: greet(to_down))

    loads = [pltpu.make_async_copy(cur_ref, buf.at[row, lag], load_sem.at[0]),
             pltpu.make_async_copy(exc_ref, exc, load_sem.at[1])]
    for r in range(rows):
        loads.append(pltpu.make_async_copy(
            pan_ref.at[0, :, pl.ds(r * width, width)], pan.at[r], load_sem.at[2 + r]))
    for load in loads:
        load.start()

    pl.semaphore_wait(barrier, 3 + has_up.astype(jnp.int32) + has_down.astype(jnp.int32))

    sent = []

    def send(src, dst, sem, device, guards=()):
        slot = len(sent)

        def make():
            return pltpu.make_async_remote_copy(
                src_ref=src(), dst_ref=dst(), send_sem=send_sem.at[slot], recv_sem=sem(),
                device_id=device, device_id_type=MESH)

        sent.append((guards, make))
        make().start()

    def place(bx, by, bz):
        return lambda: buf.at[2 * bz + by, 2 * bx + c]

    def part(bx, by, bz, h):
        return lambda: buf.at[2 * bz + by, 2 * bx + c, pl.ds(h * half, half)]

    def part_mark(bx, by, bz, h):
        return lambda: own_sem.at[((2 * bz + by) * 2 + bx) * 2 + h]

    def share_mark(bx, by, bz):
        return lambda: sib_sem.at[(2 * bz + by) * 2 + bx]

    def arrive(dst, sem):
        pltpu.make_async_remote_copy(
            src_ref=dst, dst_ref=dst, send_sem=send_sem.at[0], recv_sem=sem,
            device_id=to_s, device_id_type=MESH).wait_recv()

    def forward(bx, by, bz, h, device, guards=(), src=None):
        send(src or part(bx, by, bz, h), part(bx, by, bz, h), part_mark(bx, by, bz, h), device, guards)

    def share(bx, by, bz, guards=(), src=None):
        send(src or place(bx, by, bz), place(bx, by, bz), share_mark(bx, by, bz), to_s, guards)

    def take(bx, by, bz, h):
        arrive(part(bx, by, bz, h)(), part_mark(bx, by, bz, h)())

    def when(guard, body):
        pl.when(guard)(body)

    for h in HALVES:
        mine = lambda h=h: cur_ref.at[pl.ds(h * half, half)]
        when(has_up, lambda: forward(x, y, z, h, to_up, (has_up,), mine))
        when(has_down, lambda: forward(x, y, z, h, to_down, (has_down,), mine))
        forward(x, y, z, h, to_x, src=mine)
        forward(x, y, z, h, to_y, src=mine)
    share(x, y, z, src=lambda: cur_ref)

    acc[...] = jnp.zeros_like(acc)

    def go_on(bx, by, bz, h, up, guard):
        g, device = (has_up, to_up) if up else (has_down, to_down)
        when(g, lambda: forward(bx, by, bz, h, device, (guard, g)))

    def at_plane(up, d):
        return (z - d, z >= d) if up else (z + d, z + d < planes)

    def column(up, d, h):
        bz, guard = at_plane(up, d)

        def body():
            take(x, y, bz, h)
            if d < planes - 1:
                go_on(x, y, bz, h, up, guard)
            forward(x, y, bz, h, to_x, (guard,))
            forward(x, y, bz, h, to_y, (guard,))
            if h == 1:
                share(x, y, bz, (guard,))

        when(guard, body)

    last = planes - 1 if planes >= 3 else planes

    def diagonal(up, d, h):
        bz, guard = at_plane(up, d)

        def body():
            take(nx, ny, bz, h)
            if d + 1 < last:
                go_on(nx, ny, bz, h, up, guard)
            if h == 1:
                share(nx, ny, bz, (guard,))

        when(guard, body)

    def side(bz, guards, turn):
        take(nx, y, bz, 0)
        if turn:
            forward(nx, y, bz, 0, to_y, guards)
        take(x, ny, bz, 0)
        take(x, ny, bz, 1)
        if turn:
            forward(x, ny, bz, 1, to_x, guards)
        take(nx, y, bz, 1)
        share(nx, y, bz, guards)
        share(x, ny, bz, guards)

    def sides(up, d, h):
        bz, guard = at_plane(up, d)
        if h == 0:
            when(guard, lambda: side(bz, (guard,), d == last))

    def multiply(by, bz):
        for bx in (0, 1):
            arrive(buf.at[2 * bz + by, 2 * bx + 1 - c], share_mark(bx, by, bz)())
        r = 2 * bz + by
        lhs = buf[r].reshape(-1, width)
        acc[pl.ds(PAD, lhs.shape[0]), :] += lax.dot_general(
            lhs, pan[r], (((1,), (1,)), ((), ())), preferred_element_type=jnp.float32)

    def multiply_plane(up, d, h):
        bz, guard = at_plane(up, d)
        if h == 1:
            return

        def body():
            @pl.loop(0, 2)
            def _(by):
                multiply(by, bz)

        when(guard, body)

    def both(step, d):
        if 1 <= d < planes:
            for h in HALVES:
                step(True, d, h)
                step(False, d, h)

    side(z, (), True)
    both(column, 1)
    for h in HALVES:
        take(nx, ny, z, h)
        when(has_up, lambda: forward(nx, ny, z, h, to_up, (has_up,)))
        when(has_down, lambda: forward(nx, ny, z, h, to_down, (has_down,)))
    share(nx, ny, z)
    both(column, 2)
    if last > 1:
        both(diagonal, 1)
    for load in loads:
        load.wait()

    @pl.loop(0, 2)
    def _(by):
        multiply(by, z)

    both(column, 3)
    if last > 2:
        both(diagonal, 2)
    both(sides, 1)
    if last > 1:
        both(multiply_plane, 1)
    for d in range(2, planes):
        if d + 2 < planes:
            both(column, d + 2)
        if d + 1 < last:
            both(diagonal, d + 1)
        both(sides, d)
        if d == last:
            if d > 2:
                both(multiply_plane, d - 1)
            both(diagonal, d)
            both(multiply_plane, d)
        elif d + 1 < last:
            both(multiply_plane, d)
    piece = steps // PIECES

    def shifted(bx, core, p):
        first = pl.multiple_of(PAD - 8 + (2 * bx + core) * steps + p * piece, 8)
        window = acc[pl.ds(first, piece + 8), :]
        return pltpu.roll(window, piece + lag, 0)[:piece]

    def give_piece(j, p):
        give[j, p] = shifted(nx if j == 0 else x, 1 - c, p)
        send(lambda j=j, p=p: give.at[j, p], lambda j=j, p=p: got.at[j, p],
             lambda j=j, p=p: give_sem.at[j * PIECES + p], to_s)

    def finish(group):
        for guards, make in group:
            if guards:
                g = functools.reduce(jnp.logical_and, guards)
                pl.when(g)(lambda make=make: make().wait_send())
            else:
                make().wait_send()

    gathered = len(sent)
    for p in range(PIECES):
        give_piece(0, p)
    for p in range(PIECES):
        arrive(got.at[0, p], give_sem.at[p])
        over[p] = shifted(nx, c, p) + got[0, p]
        send(lambda p=p: over.at[p], lambda p=p: landed.at[p], lambda p=p: over_sem.at[p], to_x)
    for p in range(PIECES):
        give_piece(1, p)
    finish(sent[:gathered])
    for p in range(PIECES):
        arrive(got.at[1, p], give_sem.at[PIECES + p])
        at = pl.ds(p * piece, piece)
        exc[at, :] = exc[at, :] - (shifted(x, c, p) + got[1, p])
    for p in range(PIECES):
        arrive(landed.at[p], over_sem.at[p])
        at = pl.ds(p * piece, piece)
        out_ref[at, :] = exc[at, :] - landed[p]

    finish(sent[gathered:])


def fused(currents, panels, excitation):
    steps, width = currents.shape
    count = panels.shape[1]
    lags, rows = lax.axis_size("lag"), lax.axis_size("row")
    planes = rows // 2
    hbm_spec = pl.BlockSpec(memory_space=pltpu.HBM)
    dma = pltpu.SemaphoreType.DMA
    piece = steps // PIECES
    return pl.pallas_call(
        functools.partial(kernel, planes),
        out_shape=jax.ShapeDtypeStruct(excitation.shape, jnp.float32),
        in_specs=[hbm_spec] * 3,
        out_specs=pl.BlockSpec(memory_space=pltpu.VMEM),
        scratch_shapes=[
            pltpu.VMEM((rows, lags, steps, width), jnp.bfloat16),
            pltpu.VMEM((rows, count, width), jnp.bfloat16),
            pltpu.VMEM((steps, count), jnp.float32),
            pltpu.VMEM((PAD + lags * steps, count), jnp.float32),
            pltpu.VMEM((2, PIECES, piece, count), jnp.float32),
            pltpu.VMEM((2, PIECES, piece, count), jnp.float32),
            pltpu.VMEM((PIECES, piece, count), jnp.float32),
            pltpu.VMEM((PIECES, piece, count), jnp.float32),
            dma((24 + 32 * planes + 3 * PIECES,)),
            dma((4 * rows,)),
            dma((2 * rows,)),
            dma((2 + rows,)),
            dma((2 * PIECES,)),
            dma((PIECES,)),
        ],
        compiler_params=pltpu.CompilerParams(
            collective_id=0, has_side_effects=True, vmem_limit_bytes=64 * 2**20),
        cost_estimate=pl.CostEstimate(
            flops=2 * lags * steps * width * rows * count,
            bytes_accessed=panels.size * 2, transcendentals=0),
    )(currents, panels, excitation)


def plain(currents, panels, excitation):
    gathered = lax.all_gather(currents, "row", axis=1, tiled=True)
    block_len = currents.shape[0]
    lag_total = lax.axis_size("lag")
    lag_index = lax.axis_index("lag")
    all_times = block_len * lag_total
    running = jnp.zeros((all_times + lag_total, panels.shape[1]), jnp.float32)
    product = lax.dot_general(
        lax.all_gather(gathered, "lag", axis=0, tiled=True),
        panels[0],
        (((1,), (1,)), ((), ())),
        preferred_element_type=jnp.float32,
    )
    running = lax.dynamic_update_slice_in_dim(running, product, lag_index, 0)
    field = lax.psum_scatter(running[:all_times], "lag", scatter_dimension=0, tiled=True)
    return excitation - field


def solution(mesh):
    paired = mesh.shape["lag"] == 4 and mesh.shape["row"] % 2 == 0
    return jax.shard_map(
        fused if paired else plain,
        mesh=mesh,
        in_specs=(P("lag", "row"), P("lag", "row", None), P("lag", "row")),
        out_specs=P("lag", "row"),
        check_vma=False,
    )
```

```python
import functools

import jax
import jax.numpy as jnp
from jax import lax
from jax.experimental import pallas as pl
from jax.experimental.pallas import tpu as pltpu
from jax.sharding import PartitionSpec as P

MESH = pl.DeviceIdType.MESH
PAD = 16
PIECES = 4
HALVES = (0, 1)


def kernel(planes, cur_ref, pan_ref, exc_ref, out_ref, buf, pan, exc, acc, give, got, over, landed,
           send_sem, own_sem, sib_sem, load_sem, give_sem, over_sem):
    lag, row = lax.axis_index("lag"), lax.axis_index("row")
    x, c = lag // 2, lag % 2
    z, y = row // 2, row % 2
    nx, ny = 1 - x, 1 - y
    steps, width = cur_ref.shape
    rows = 2 * planes
    half = steps // 2
    to_x, to_y = (2 * nx + c, row), (lag, 2 * z + ny)
    to_s = (2 * x + 1 - c, row)
    to_up, to_down = (lag, row + 2), (lag, row - 2)
    has_up, has_down = z + 1 < planes, z >= 1

    barrier = pltpu.get_barrier_semaphore()

    def greet(device):
        pl.semaphore_signal(barrier, inc=1, device_id=device, device_id_type=MESH)

    greet(to_s)
    greet(to_x)
    greet(to_y)
    pl.when(has_up)(lambda: greet(to_up))
    pl.when(has_down)(lambda: greet(to_down))

    loads = [pltpu.make_async_copy(cur_ref, buf.at[row, lag], load_sem.at[0]),
             pltpu.make_async_copy(exc_ref, exc, load_sem.at[1])]
    for r in range(rows):
        loads.append(pltpu.make_async_copy(
            pan_ref.at[0, :, pl.ds(r * width, width)], pan.at[r], load_sem.at[2 + r]))
    for load in loads:
        load.start()

    pl.semaphore_wait(barrier, 3 + has_up.astype(jnp.int32) + has_down.astype(jnp.int32))

    sent = []

    def send(src, dst, sem, device, guards=()):
        slot = len(sent)

        def make():
            return pltpu.make_async_remote_copy(
                src_ref=src(), dst_ref=dst(), send_sem=send_sem.at[slot], recv_sem=sem(),
                device_id=device, device_id_type=MESH)

        sent.append((guards, make))
        make().start()

    def place(bx, by, bz):
        return lambda: buf.at[2 * bz + by, 2 * bx + c]

    def part(bx, by, bz, h):
        return lambda: buf.at[2 * bz + by, 2 * bx + c, pl.ds(h * half, half)]

    def part_mark(bx, by, bz, h):
        return lambda: own_sem.at[((2 * bz + by) * 2 + bx) * 2 + h]

    def share_mark(bx, by, bz):
        return lambda: sib_sem.at[(2 * bz + by) * 2 + bx]

    def arrive(dst, sem):
        pltpu.make_async_remote_copy(
            src_ref=dst, dst_ref=dst, send_sem=send_sem.at[0], recv_sem=sem,
            device_id=to_s, device_id_type=MESH).wait_recv()

    def forward(bx, by, bz, h, device, guards=(), src=None):
        send(src or part(bx, by, bz, h), part(bx, by, bz, h), part_mark(bx, by, bz, h), device, guards)

    def share(bx, by, bz, guards=(), src=None):
        send(src or place(bx, by, bz), place(bx, by, bz), share_mark(bx, by, bz), to_s, guards)

    def take(bx, by, bz, h):
        arrive(part(bx, by, bz, h)(), part_mark(bx, by, bz, h)())

    def when(guard, body):
        pl.when(guard)(body)

    for h in HALVES:
        mine = lambda h=h: cur_ref.at[pl.ds(h * half, half)]
        when(has_up, lambda: forward(x, y, z, h, to_up, (has_up,), mine))
        when(has_down, lambda: forward(x, y, z, h, to_down, (has_down,), mine))
        forward(x, y, z, h, to_x, src=mine)
        forward(x, y, z, h, to_y, src=mine)
    share(x, y, z, src=lambda: cur_ref)

    acc[...] = jnp.zeros_like(acc)

    def go_on(bx, by, bz, h, up, guard):
        g, device = (has_up, to_up) if up else (has_down, to_down)
        when(g, lambda: forward(bx, by, bz, h, device, (guard, g)))

    def at_plane(up, d):
        return (z - d, z >= d) if up else (z + d, z + d < planes)

    def column(up, d, h):
        bz, guard = at_plane(up, d)

        def body():
            take(x, y, bz, h)
            if d < planes - 1:
                go_on(x, y, bz, h, up, guard)
            forward(x, y, bz, h, to_x, (guard,))
            forward(x, y, bz, h, to_y, (guard,))
            if h == 1:
                share(x, y, bz, (guard,))

        when(guard, body)

    last = planes - 1 if planes >= 3 else planes

    def diagonal(up, d, h):
        bz, guard = at_plane(up, d)

        def body():
            take(nx, ny, bz, h)
            if d + 1 < last or (d + 1 == last and h == 1 and last < planes):
                go_on(nx, ny, bz, h, up, guard)
            if h == 1:
                share(nx, ny, bz, (guard,))

        when(guard, body)

    def side(bz, guards, over_x, over_y):
        take(nx, y, bz, 0)
        if over_y:
            forward(nx, y, bz, 0, to_y, guards)
        take(x, ny, bz, 0)
        take(x, ny, bz, 1)
        if over_x:
            forward(x, ny, bz, 1, to_x, guards)
        take(nx, y, bz, 1)
        share(nx, y, bz, guards)
        share(x, ny, bz, guards)

    def sides(up, d, h):
        bz, guard = at_plane(up, d)
        if h == 0:
            when(guard, lambda: side(bz, (guard,), False, d == last))

    def multiply(by, bz):
        for bx in (0, 1):
            arrive(buf.at[2 * bz + by, 2 * bx + 1 - c], share_mark(bx, by, bz)())
        r = 2 * bz + by
        lhs = buf[r].reshape(-1, width)
        acc[pl.ds(PAD, lhs.shape[0]), :] += lax.dot_general(
            lhs, pan[r], (((1,), (1,)), ((), ())), preferred_element_type=jnp.float32)

    def multiply_near(up, d, h):
        bz, guard = at_plane(up, d)
        if h == 0:
            when(guard, lambda: multiply(y, bz))

    def multiply_far(up, d, h):
        bz, guard = at_plane(up, d)
        if h == 0:
            when(guard, lambda: multiply(ny, bz))

    def both(step, d):
        if 1 <= d < planes:
            for h in HALVES:
                step(True, d, h)
                step(False, d, h)

    side(z, (), True, True)
    both(column, 1)
    both(column, 2)
    for h in HALVES:
        take(nx, ny, z, h)
        when(has_up, lambda: forward(nx, ny, z, h, to_up, (has_up,)))
        when(has_down, lambda: forward(nx, ny, z, h, to_down, (has_down,)))
    share(nx, ny, z)
    if last > 1:
        both(diagonal, 1)
    for load in loads:
        load.wait()
    multiply(y, z)
    both(column, 3)
    multiply(ny, z)
    both(sides, 1)
    both(multiply_near, 1)
    if last > 2:
        both(diagonal, 2)
    if last > 1:
        both(multiply_far, 1)
    for d in range(2, planes):
        if d + 2 < planes:
            both(column, d + 2)
        if 2 < d + 1 < last:
            both(diagonal, d + 1)
        if d < last or d == 2:
            both(sides, d)
        if d < last:
            if d + 1 == last:
                both(sides, d + 1)
            both(multiply_near, d)
            both(multiply_far, d)
        else:
            both(multiply_near, d)
            both(diagonal, d)
            both(multiply_far, d)

    piece = steps // PIECES

    def shifted(bx, core, p):
        first = pl.multiple_of(PAD - 8 + (2 * bx + core) * steps + p * piece, 8)
        window = acc[pl.ds(first, piece + 8), :]
        return pltpu.roll(window, piece + lag, 0)[:piece]

    def give_piece(j, p):
        give[j, p] = shifted(nx if j == 0 else x, 1 - c, p)
        send(lambda j=j, p=p: give.at[j, p], lambda j=j, p=p: got.at[j, p],
             lambda j=j, p=p: give_sem.at[j * PIECES + p], to_s)

    def finish(group):
        for guards, make in group:
            if guards:
                g = functools.reduce(jnp.logical_and, guards)
                pl.when(g)(lambda make=make: make().wait_send())
            else:
                make().wait_send()

    gathered = len(sent)
    for p in range(PIECES):
        give_piece(0, p)
    for p in range(PIECES):
        arrive(got.at[0, p], give_sem.at[p])
        over[p] = shifted(nx, c, p) + got[0, p]
        send(lambda p=p: over.at[p], lambda p=p: landed.at[p], lambda p=p: over_sem.at[p], to_x)
    for p in range(PIECES):
        give_piece(1, p)
    finish(sent[:gathered])
    for p in range(PIECES):
        arrive(got.at[1, p], give_sem.at[PIECES + p])
        at = pl.ds(p * piece, piece)
        exc[at, :] = exc[at, :] - (shifted(x, c, p) + got[1, p])
    for p in range(PIECES):
        arrive(landed.at[p], over_sem.at[p])
        at = pl.ds(p * piece, piece)
        out_ref[at, :] = exc[at, :] - landed[p]

    finish(sent[gathered:])


def fused(currents, panels, excitation):
    steps, width = currents.shape
    count = panels.shape[1]
    lags, rows = lax.axis_size("lag"), lax.axis_size("row")
    planes = rows // 2
    hbm_spec = pl.BlockSpec(memory_space=pltpu.HBM)
    dma = pltpu.SemaphoreType.DMA
    piece = steps // PIECES
    return pl.pallas_call(
        functools.partial(kernel, planes),
        out_shape=jax.ShapeDtypeStruct(excitation.shape, jnp.float32),
        in_specs=[hbm_spec] * 3,
        out_specs=pl.BlockSpec(memory_space=pltpu.VMEM),
        scratch_shapes=[
            pltpu.VMEM((rows, lags, steps, width), jnp.bfloat16),
            pltpu.VMEM((rows, count, width), jnp.bfloat16),
            pltpu.VMEM((steps, count), jnp.float32),
            pltpu.VMEM((PAD + lags * steps, count), jnp.float32),
            pltpu.VMEM((2, PIECES, piece, count), jnp.float32),
            pltpu.VMEM((2, PIECES, piece, count), jnp.float32),
            pltpu.VMEM((PIECES, piece, count), jnp.float32),
            pltpu.VMEM((PIECES, piece, count), jnp.float32),
            dma((24 + 32 * planes + 3 * PIECES,)),
            dma((4 * rows,)),
            dma((2 * rows,)),
            dma((2 + rows,)),
            dma((2 * PIECES,)),
            dma((PIECES,)),
        ],
        compiler_params=pltpu.CompilerParams(
            collective_id=0, has_side_effects=True, vmem_limit_bytes=64 * 2**20),
        cost_estimate=pl.CostEstimate(
            flops=2 * lags * steps * width * rows * count,
            bytes_accessed=panels.size * 2, transcendentals=0),
    )(currents, panels, excitation)


def plain(currents, panels, excitation):
    gathered = lax.all_gather(currents, "row", axis=1, tiled=True)
    block_len = currents.shape[0]
    lag_total = lax.axis_size("lag")
    lag_index = lax.axis_index("lag")
    all_times = block_len * lag_total
    running = jnp.zeros((all_times + lag_total, panels.shape[1]), jnp.float32)
    product = lax.dot_general(
        lax.all_gather(gathered, "lag", axis=0, tiled=True),
        panels[0],
        (((1,), (1,)), ((), ())),
        preferred_element_type=jnp.float32,
    )
    running = lax.dynamic_update_slice_in_dim(running, product, lag_index, 0)
    field = lax.psum_scatter(running[:all_times], "lag", scatter_dimension=0, tiled=True)
    return excitation - field


def solution(mesh):
    paired = mesh.shape["lag"] == 4 and mesh.shape["row"] % 2 == 0
    return jax.shard_map(
        fused if paired else plain,
        mesh=mesh,
        in_specs=(P("lag", "row"), P("lag", "row", None), P("lag", "row")),
        out_specs=P("lag", "row"),
        check_vma=False,
    )
```

```python
import functools

import jax
import jax.numpy as jnp
from jax import lax
from jax.experimental import pallas as pl
from jax.experimental.pallas import tpu as pltpu
from jax.sharding import PartitionSpec as P

MESH = pl.DeviceIdType.MESH
PAD = 16
PIECES = 4
HALVES = (0, 1)


def kernel(planes, cur_ref, pan_ref, exc_ref, out_ref, buf, pan, exc, acc, give, got, over, landed,
           send_sem, own_sem, sib_sem, load_sem, give_sem, over_sem):
    lag, row = lax.axis_index("lag"), lax.axis_index("row")
    x, c = lag // 2, lag % 2
    z, y = row // 2, row % 2
    nx, ny = 1 - x, 1 - y
    steps, width = cur_ref.shape
    rows = 2 * planes
    half = steps // 2
    to_x, to_y = (2 * nx + c, row), (lag, 2 * z + ny)
    to_s = (2 * x + 1 - c, row)
    to_up, to_down = (lag, row + 2), (lag, row - 2)
    has_up, has_down = z + 1 < planes, z >= 1

    barrier = pltpu.get_barrier_semaphore()

    def greet(device):
        pl.semaphore_signal(barrier, inc=1, device_id=device, device_id_type=MESH)

    greet(to_s)
    greet(to_x)
    greet(to_y)
    pl.when(has_up)(lambda: greet(to_up))
    pl.when(has_down)(lambda: greet(to_down))

    loads = [pltpu.make_async_copy(cur_ref, buf.at[row, lag], load_sem.at[0]),
             pltpu.make_async_copy(exc_ref, exc, load_sem.at[1])]
    for r in range(rows):
        loads.append(pltpu.make_async_copy(
            pan_ref.at[0, :, pl.ds(r * width, width)], pan.at[r], load_sem.at[2 + r]))
    for load in loads:
        load.start()

    pl.semaphore_wait(barrier, 3 + has_up.astype(jnp.int32) + has_down.astype(jnp.int32))

    sent = []

    def send(src, dst, sem, device, guards=()):
        slot = len(sent)

        def make():
            return pltpu.make_async_remote_copy(
                src_ref=src(), dst_ref=dst(), send_sem=send_sem.at[slot], recv_sem=sem(),
                device_id=device, device_id_type=MESH)

        sent.append((guards, make))
        make().start()

    def place(bx, by, bz):
        return lambda: buf.at[2 * bz + by, 2 * bx + c]

    def part(bx, by, bz, h):
        return lambda: buf.at[2 * bz + by, 2 * bx + c, pl.ds(h * half, half)]

    def part_mark(bx, by, bz, h):
        return lambda: own_sem.at[((2 * bz + by) * 2 + bx) * 2 + h]

    def share_mark(bx, by, bz):
        return lambda: sib_sem.at[(2 * bz + by) * 2 + bx]

    def arrive(dst, sem):
        pltpu.make_async_remote_copy(
            src_ref=dst, dst_ref=dst, send_sem=send_sem.at[0], recv_sem=sem,
            device_id=to_s, device_id_type=MESH).wait_recv()

    def forward(bx, by, bz, h, device, guards=(), src=None):
        send(src or part(bx, by, bz, h), part(bx, by, bz, h), part_mark(bx, by, bz, h), device, guards)

    def share(bx, by, bz, guards=(), src=None):
        send(src or place(bx, by, bz), place(bx, by, bz), share_mark(bx, by, bz), to_s, guards)

    def take(bx, by, bz, h):
        arrive(part(bx, by, bz, h)(), part_mark(bx, by, bz, h)())

    def when(guard, body):
        pl.when(guard)(body)

    for h in HALVES:
        mine = lambda h=h: cur_ref.at[pl.ds(h * half, half)]
        when(has_up, lambda: forward(x, y, z, h, to_up, (has_up,), mine))
        when(has_down, lambda: forward(x, y, z, h, to_down, (has_down,), mine))
        forward(x, y, z, h, to_x, src=mine)
        forward(x, y, z, h, to_y, src=mine)
    share(x, y, z, src=lambda: cur_ref)

    acc[...] = jnp.zeros_like(acc)

    def go_on(bx, by, bz, h, up, guard):
        g, device = (has_up, to_up) if up else (has_down, to_down)
        when(g, lambda: forward(bx, by, bz, h, device, (guard, g)))

    def at_plane(up, d):
        return (z - d, z >= d) if up else (z + d, z + d < planes)

    def column(up, d, h):
        bz, guard = at_plane(up, d)

        def body():
            take(x, y, bz, h)
            if d < planes - 1:
                go_on(x, y, bz, h, up, guard)
            forward(x, y, bz, h, to_x, (guard,))
            forward(x, y, bz, h, to_y, (guard,))
            if h == 1:
                share(x, y, bz, (guard,))

        when(guard, body)

    last = planes - 1 if planes >= 3 else planes

    def diagonal(up, d, h):
        bz, guard = at_plane(up, d)

        def body():
            take(nx, ny, bz, h)
            if d + 1 < last or (d + 1 == last and h == 1 and last < planes):
                go_on(nx, ny, bz, h, up, guard)
            if h == 1:
                share(nx, ny, bz, (guard,))

        when(guard, body)

    def side(bz, guards, halves):
        for h in HALVES:
            take(nx, y, bz, h)
            if h in halves:
                forward(nx, y, bz, h, to_y, guards)
        share(nx, y, bz, guards)
        take(x, ny, bz, 0)
        take(x, ny, bz, 1)
        share(x, ny, bz, guards)

    def sides(up, d, h):
        bz, guard = at_plane(up, d)
        if h == 0:
            when(guard, lambda: side(bz, (guard,), (0,) if d == last else ()))

    def multiply(by, bz):
        for bx in (0, 1):
            arrive(buf.at[2 * bz + by, 2 * bx + 1 - c], share_mark(bx, by, bz)())
        r = 2 * bz + by
        lhs = buf[r].reshape(-1, width)
        acc[pl.ds(PAD, lhs.shape[0]), :] += lax.dot_general(
            lhs, pan[r], (((1,), (1,)), ((), ())), preferred_element_type=jnp.float32)

    def multiply_near(up, d, h):
        bz, guard = at_plane(up, d)
        if h == 0:
            when(guard, lambda: multiply(y, bz))

    def multiply_far(up, d, h):
        bz, guard = at_plane(up, d)
        if h == 0:
            when(guard, lambda: multiply(ny, bz))

    def both(step, d):
        if 1 <= d < planes:
            for h in HALVES:
                step(True, d, h)
                step(False, d, h)

    side(z, (), HALVES)
    both(column, 1)
    both(column, 2)
    for h in HALVES:
        take(nx, ny, z, h)
        when(has_up, lambda: forward(nx, ny, z, h, to_up, (has_up,)))
        when(has_down, lambda: forward(nx, ny, z, h, to_down, (has_down,)))
    share(nx, ny, z)
    if last > 1:
        both(diagonal, 1)
    for load in loads:
        load.wait()
    multiply(y, z)
    both(column, 3)
    multiply(ny, z)
    both(sides, 1)
    both(multiply_near, 1)
    if last > 2:
        both(diagonal, 2)
    if last > 1:
        both(multiply_far, 1)
    for d in range(2, planes):
        if d + 2 < planes:
            both(column, d + 2)
        if 2 < d + 1 < last:
            both(diagonal, d + 1)
        if d < last or d == 2:
            both(sides, d)
        if d < last:
            if d + 1 == last:
                both(sides, d + 1)
            both(multiply_near, d)
            both(multiply_far, d)
        else:
            both(multiply_near, d)
            both(diagonal, d)
            both(multiply_far, d)

    piece = steps // PIECES

    def shifted(bx, core, p):
        first = pl.multiple_of(PAD - 8 + (2 * bx + core) * steps + p * piece, 8)
        window = acc[pl.ds(first, piece + 8), :]
        return pltpu.roll(window, piece + lag, 0)[:piece]

    def give_piece(j, p):
        give[j, p] = shifted(nx if j == 0 else x, 1 - c, p)
        send(lambda j=j, p=p: give.at[j, p], lambda j=j, p=p: got.at[j, p],
             lambda j=j, p=p: give_sem.at[j * PIECES + p], to_s)

    def finish(group):
        for guards, make in group:
            if guards:
                g = functools.reduce(jnp.logical_and, guards)
                pl.when(g)(lambda make=make: make().wait_send())
            else:
                make().wait_send()

    gathered = len(sent)
    for p in range(PIECES):
        give_piece(0, p)
    for p in range(PIECES):
        arrive(got.at[0, p], give_sem.at[p])
        over[p] = shifted(nx, c, p) + got[0, p]
        send(lambda p=p: over.at[p], lambda p=p: landed.at[p], lambda p=p: over_sem.at[p], to_x)
    for p in range(PIECES):
        give_piece(1, p)
    finish(sent[:gathered])
    for p in range(PIECES):
        arrive(got.at[1, p], give_sem.at[PIECES + p])
        at = pl.ds(p * piece, piece)
        exc[at, :] = exc[at, :] - (shifted(x, c, p) + got[1, p])
    for p in range(PIECES):
        arrive(landed.at[p], over_sem.at[p])
        at = pl.ds(p * piece, piece)
        out_ref[at, :] = exc[at, :] - landed[p]

    finish(sent[gathered:])


def fused(currents, panels, excitation):
    steps, width = currents.shape
    count = panels.shape[1]
    lags, rows = lax.axis_size("lag"), lax.axis_size("row")
    planes = rows // 2
    hbm_spec = pl.BlockSpec(memory_space=pltpu.HBM)
    dma = pltpu.SemaphoreType.DMA
    piece = steps // PIECES
    return pl.pallas_call(
        functools.partial(kernel, planes),
        out_shape=jax.ShapeDtypeStruct(excitation.shape, jnp.float32),
        in_specs=[hbm_spec] * 3,
        out_specs=pl.BlockSpec(memory_space=pltpu.VMEM),
        scratch_shapes=[
            pltpu.VMEM((rows, lags, steps, width), jnp.bfloat16),
            pltpu.VMEM((rows, count, width), jnp.bfloat16),
            pltpu.VMEM((steps, count), jnp.float32),
            pltpu.VMEM((PAD + lags * steps, count), jnp.float32),
            pltpu.VMEM((2, PIECES, piece, count), jnp.float32),
            pltpu.VMEM((2, PIECES, piece, count), jnp.float32),
            pltpu.VMEM((PIECES, piece, count), jnp.float32),
            pltpu.VMEM((PIECES, piece, count), jnp.float32),
            dma((24 + 32 * planes + 3 * PIECES,)),
            dma((4 * rows,)),
            dma((2 * rows,)),
            dma((2 + rows,)),
            dma((2 * PIECES,)),
            dma((PIECES,)),
        ],
        compiler_params=pltpu.CompilerParams(
            collective_id=0, has_side_effects=True, vmem_limit_bytes=64 * 2**20),
        cost_estimate=pl.CostEstimate(
            flops=2 * lags * steps * width * rows * count,
            bytes_accessed=panels.size * 2, transcendentals=0),
    )(currents, panels, excitation)


def plain(currents, panels, excitation):
    gathered = lax.all_gather(currents, "row", axis=1, tiled=True)
    block_len = currents.shape[0]
    lag_total = lax.axis_size("lag")
    lag_index = lax.axis_index("lag")
    all_times = block_len * lag_total
    running = jnp.zeros((all_times + lag_total, panels.shape[1]), jnp.float32)
    product = lax.dot_general(
        lax.all_gather(gathered, "lag", axis=0, tiled=True),
        panels[0],
        (((1,), (1,)), ((), ())),
        preferred_element_type=jnp.float32,
    )
    running = lax.dynamic_update_slice_in_dim(running, product, lag_index, 0)
    field = lax.psum_scatter(running[:all_times], "lag", scatter_dimension=0, tiled=True)
    return excitation - field


def solution(mesh):
    paired = mesh.shape["lag"] == 4 and mesh.shape["row"] % 2 == 0
    return jax.shard_map(
        fused if paired else plain,
        mesh=mesh,
        in_specs=(P("lag", "row"), P("lag", "row", None), P("lag", "row")),
        out_specs=P("lag", "row"),
        check_vma=False,
    )
```

```python
import functools

import jax
import jax.numpy as jnp
from jax import lax
from jax.experimental import pallas as pl
from jax.experimental.pallas import tpu as pltpu
from jax.sharding import PartitionSpec as P

MESH = pl.DeviceIdType.MESH
PAD = 16
PIECES = 4
HALVES = (0, 1)


def kernel(planes, cur_ref, pan_ref, exc_ref, out_ref, buf, pan, exc, acc, give, got, over, landed,
           send_sem, own_sem, sib_sem, load_sem, give_sem, over_sem):
    lag, row = lax.axis_index("lag"), lax.axis_index("row")
    x, c = lag // 2, lag % 2
    z, y = row // 2, row % 2
    nx, ny = 1 - x, 1 - y
    steps, width = cur_ref.shape
    rows = 2 * planes
    half = steps // 2
    to_x, to_y = (2 * nx + c, row), (lag, 2 * z + ny)
    to_s = (2 * x + 1 - c, row)
    to_up, to_down = (lag, row + 2), (lag, row - 2)
    has_up, has_down = z + 1 < planes, z >= 1
    direct = planes >= 4
    at_end = jnp.logical_or(z == 0, z == planes - 1)
    to_end = (lag, 2 * (planes - 1 - z) + y)

    barrier = pltpu.get_barrier_semaphore()

    def greet(device):
        pl.semaphore_signal(barrier, inc=1, device_id=device, device_id_type=MESH)

    greet(to_s)
    greet(to_x)
    greet(to_y)
    pl.when(has_up)(lambda: greet(to_up))
    pl.when(has_down)(lambda: greet(to_down))
    if direct:
        pl.when(at_end)(lambda: greet(to_end))

    loads = [pltpu.make_async_copy(cur_ref, buf.at[row, lag], load_sem.at[0]),
             pltpu.make_async_copy(exc_ref, exc, load_sem.at[1])]
    for r in range(rows):
        loads.append(pltpu.make_async_copy(
            pan_ref.at[0, :, pl.ds(r * width, width)], pan.at[r], load_sem.at[2 + r]))
    for load in loads:
        load.start()

    greeted = 3 + has_up.astype(jnp.int32) + has_down.astype(jnp.int32)
    pl.semaphore_wait(barrier, greeted + at_end.astype(jnp.int32) if direct else greeted)

    sent = []

    def send(src, dst, sem, device, guards=()):
        slot = len(sent)

        def make():
            return pltpu.make_async_remote_copy(
                src_ref=src(), dst_ref=dst(), send_sem=send_sem.at[slot], recv_sem=sem(),
                device_id=device, device_id_type=MESH)

        sent.append((guards, make))
        make().start()

    def place(bx, by, bz):
        return lambda: buf.at[2 * bz + by, 2 * bx + c]

    def part(bx, by, bz, h):
        return lambda: buf.at[2 * bz + by, 2 * bx + c, pl.ds(h * half, half)]

    def part_mark(bx, by, bz, h):
        return lambda: own_sem.at[((2 * bz + by) * 2 + bx) * 2 + h]

    def share_mark(bx, by, bz):
        return lambda: sib_sem.at[(2 * bz + by) * 2 + bx]

    def arrive(dst, sem):
        pltpu.make_async_remote_copy(
            src_ref=dst, dst_ref=dst, send_sem=send_sem.at[0], recv_sem=sem,
            device_id=to_s, device_id_type=MESH).wait_recv()

    def forward(bx, by, bz, h, device, guards=(), src=None):
        send(src or part(bx, by, bz, h), part(bx, by, bz, h), part_mark(bx, by, bz, h), device, guards)

    def share(bx, by, bz, guards=(), src=None):
        send(src or place(bx, by, bz), place(bx, by, bz), share_mark(bx, by, bz), to_s, guards)

    def take(bx, by, bz, h):
        arrive(part(bx, by, bz, h)(), part_mark(bx, by, bz, h)())

    def when(guard, body):
        pl.when(guard)(body)

    for h in HALVES:
        mine = lambda h=h: cur_ref.at[pl.ds(h * half, half)]
        when(has_up, lambda: forward(x, y, z, h, to_up, (has_up,), mine))
        when(has_down, lambda: forward(x, y, z, h, to_down, (has_down,), mine))
        if direct:
            when(at_end, lambda: forward(x, y, z, h, to_end, (at_end,), mine))
        forward(x, y, z, h, to_x, src=mine)
        forward(x, y, z, h, to_y, src=mine)
    share(x, y, z, src=lambda: cur_ref)

    acc[...] = jnp.zeros_like(acc)

    def go_on(bx, by, bz, h, up, guard):
        g, device = (has_up, to_up) if up else (has_down, to_down)
        when(g, lambda: forward(bx, by, bz, h, device, (guard, g)))

    def at_plane(up, d):
        return (z - d, z >= d) if up else (z + d, z + d < planes)

    def column(up, d, h):
        bz, guard = at_plane(up, d)

        def body():
            take(x, y, bz, h)
            if d < planes - (2 if direct else 1):
                go_on(x, y, bz, h, up, guard)
            forward(x, y, bz, h, to_x, (guard,))
            forward(x, y, bz, h, to_y, (guard,))
            if h == 1:
                share(x, y, bz, (guard,))

        when(guard, body)

    last = planes - 1 if planes >= 3 else planes

    def diagonal(up, d, h):
        bz, guard = at_plane(up, d)

        def body():
            take(nx, ny, bz, h)
            if d + 1 < last or (d + 1 == last and h == 1 and last < planes):
                go_on(nx, ny, bz, h, up, guard)
            if h == 1:
                share(nx, ny, bz, (guard,))

        when(guard, body)

    def side(bz, guards, over_x, over_y):
        take(nx, y, bz, 0)
        if over_y:
            forward(nx, y, bz, 0, to_y, guards)
        take(x, ny, bz, 0)
        take(x, ny, bz, 1)
        if over_x:
            forward(x, ny, bz, 1, to_x, guards)
        take(nx, y, bz, 1)
        share(nx, y, bz, guards)
        share(x, ny, bz, guards)

    def sides(up, d, h):
        bz, guard = at_plane(up, d)
        if h == 0:
            when(guard, lambda: side(bz, (guard,), False, d == last))

    def multiply(by, bz):
        for bx in (0, 1):
            arrive(buf.at[2 * bz + by, 2 * bx + 1 - c], share_mark(bx, by, bz)())
        r = 2 * bz + by
        lhs = buf[r].reshape(-1, width)
        acc[pl.ds(PAD, lhs.shape[0]), :] += lax.dot_general(
            lhs, pan[r], (((1,), (1,)), ((), ())), preferred_element_type=jnp.float32)

    def multiply_near(up, d, h):
        bz, guard = at_plane(up, d)
        if h == 0:
            when(guard, lambda: multiply(y, bz))

    def multiply_far(up, d, h):
        bz, guard = at_plane(up, d)
        if h == 0:
            when(guard, lambda: multiply(ny, bz))

    def both(step, d):
        if 1 <= d < planes:
            for h in HALVES:
                step(True, d, h)
                step(False, d, h)

    side(z, (), True, True)
    both(column, 1)
    for d in range(2, planes):
        both(column, d)
    for h in HALVES:
        take(nx, ny, z, h)
        when(has_up, lambda: forward(nx, ny, z, h, to_up, (has_up,)))
        when(has_down, lambda: forward(nx, ny, z, h, to_down, (has_down,)))
    share(nx, ny, z)
    if last > 1:
        both(diagonal, 1)
    for load in loads:
        load.wait()
    multiply(y, z)
    both(sides, 1)
    multiply(ny, z)
    for d in range(2, last):
        both(diagonal, d)
    for d in range(2, planes):
        both(sides, d)
        both(multiply_near, d - 1)
        both(multiply_far, d - 1)
    if planes > 1:
        both(multiply_near, planes - 1)
        if last < planes:
            both(diagonal, last)
        both(multiply_far, planes - 1)

    piece = steps // PIECES

    def shifted(bx, core, p):
        first = pl.multiple_of(PAD - 8 + (2 * bx + core) * steps + p * piece, 8)
        window = acc[pl.ds(first, piece + 8), :]
        return pltpu.roll(window, piece + lag, 0)[:piece]

    def give_piece(j, p):
        give[j, p] = shifted(nx if j == 0 else x, 1 - c, p)
        send(lambda j=j, p=p: give.at[j, p], lambda j=j, p=p: got.at[j, p],
             lambda j=j, p=p: give_sem.at[j * PIECES + p], to_s)

    def finish(group):
        for guards, make in group:
            if guards:
                g = functools.reduce(jnp.logical_and, guards)
                pl.when(g)(lambda make=make: make().wait_send())
            else:
                make().wait_send()

    gathered = len(sent)
    for p in range(PIECES):
        give_piece(0, p)
    for p in range(PIECES):
        arrive(got.at[0, p], give_sem.at[p])
        over[p] = shifted(nx, c, p) + got[0, p]
        send(lambda p=p: over.at[p], lambda p=p: landed.at[p], lambda p=p: over_sem.at[p], to_x)
    for p in range(PIECES):
        give_piece(1, p)
    finish(sent[:gathered])
    for p in range(PIECES):
        arrive(got.at[1, p], give_sem.at[PIECES + p])
        at = pl.ds(p * piece, piece)
        exc[at, :] = exc[at, :] - (shifted(x, c, p) + got[1, p])
    for p in range(PIECES):
        arrive(landed.at[p], over_sem.at[p])
        at = pl.ds(p * piece, piece)
        out_ref[at, :] = exc[at, :] - landed[p]

    finish(sent[gathered:])


def fused(currents, panels, excitation):
    steps, width = currents.shape
    count = panels.shape[1]
    lags, rows = lax.axis_size("lag"), lax.axis_size("row")
    planes = rows // 2
    hbm_spec = pl.BlockSpec(memory_space=pltpu.HBM)
    dma = pltpu.SemaphoreType.DMA
    piece = steps // PIECES
    return pl.pallas_call(
        functools.partial(kernel, planes),
        out_shape=jax.ShapeDtypeStruct(excitation.shape, jnp.float32),
        in_specs=[hbm_spec] * 3,
        out_specs=pl.BlockSpec(memory_space=pltpu.VMEM),
        scratch_shapes=[
            pltpu.VMEM((rows, lags, steps, width), jnp.bfloat16),
            pltpu.VMEM((rows, count, width), jnp.bfloat16),
            pltpu.VMEM((steps, count), jnp.float32),
            pltpu.VMEM((PAD + lags * steps, count), jnp.float32),
            pltpu.VMEM((2, PIECES, piece, count), jnp.float32),
            pltpu.VMEM((2, PIECES, piece, count), jnp.float32),
            pltpu.VMEM((PIECES, piece, count), jnp.float32),
            pltpu.VMEM((PIECES, piece, count), jnp.float32),
            dma((26 + 32 * planes + 3 * PIECES,)),
            dma((4 * rows,)),
            dma((2 * rows,)),
            dma((2 + rows,)),
            dma((2 * PIECES,)),
            dma((PIECES,)),
        ],
        compiler_params=pltpu.CompilerParams(
            collective_id=0, has_side_effects=True, vmem_limit_bytes=64 * 2**20),
        cost_estimate=pl.CostEstimate(
            flops=2 * lags * steps * width * rows * count,
            bytes_accessed=panels.size * 2, transcendentals=0),
    )(currents, panels, excitation)


def plain(currents, panels, excitation):
    gathered = lax.all_gather(currents, "row", axis=1, tiled=True)
    block_len = currents.shape[0]
    lag_total = lax.axis_size("lag")
    lag_index = lax.axis_index("lag")
    all_times = block_len * lag_total
    running = jnp.zeros((all_times + lag_total, panels.shape[1]), jnp.float32)
    product = lax.dot_general(
        lax.all_gather(gathered, "lag", axis=0, tiled=True),
        panels[0],
        (((1,), (1,)), ((), ())),
        preferred_element_type=jnp.float32,
    )
    running = lax.dynamic_update_slice_in_dim(running, product, lag_index, 0)
    field = lax.psum_scatter(running[:all_times], "lag", scatter_dimension=0, tiled=True)
    return excitation - field


def solution(mesh):
    paired = mesh.shape["lag"] == 4 and mesh.shape["row"] % 2 == 0
    return jax.shard_map(
        fused if paired else plain,
        mesh=mesh,
        in_specs=(P("lag", "row"), P("lag", "row", None), P("lag", "row")),
        out_specs=P("lag", "row"),
        check_vma=False,
    )
```

```python
import functools

import jax
import jax.numpy as jnp
from jax import lax
from jax.experimental import pallas as pl
from jax.experimental.pallas import tpu as pltpu
from jax.sharding import PartitionSpec as P

MESH = pl.DeviceIdType.MESH
PAD = 16
PIECES = 4
HALVES = (0, 1)


def kernel(planes, cur_ref, pan_ref, exc_ref, out_ref, buf, pan, exc, acc, give, got, over, landed,
           send_sem, own_sem, sib_sem, load_sem, give_sem, over_sem):
    lag, row = lax.axis_index("lag"), lax.axis_index("row")
    x, c = lag // 2, lag % 2
    z, y = row // 2, row % 2
    nx, ny = 1 - x, 1 - y
    steps, width = cur_ref.shape
    rows = 2 * planes
    half = steps // 2
    to_x, to_y = (2 * nx + c, row), (lag, 2 * z + ny)
    to_s = (2 * x + 1 - c, row)
    to_up, to_down = (lag, row + 2), (lag, row - 2)
    has_up, has_down = z + 1 < planes, z >= 1
    direct = planes >= 4
    at_end = jnp.logical_or(z == 0, z == planes - 1)
    to_end = (lag, 2 * (planes - 1 - z) + y)

    barrier = pltpu.get_barrier_semaphore()

    def greet(device):
        pl.semaphore_signal(barrier, inc=1, device_id=device, device_id_type=MESH)

    greet(to_s)
    greet(to_x)
    greet(to_y)
    pl.when(has_up)(lambda: greet(to_up))
    pl.when(has_down)(lambda: greet(to_down))
    if direct:
        pl.when(at_end)(lambda: greet(to_end))

    loads = [pltpu.make_async_copy(cur_ref, buf.at[row, lag], load_sem.at[0]),
             pltpu.make_async_copy(exc_ref, exc, load_sem.at[1])]
    for r in range(rows):
        loads.append(pltpu.make_async_copy(
            pan_ref.at[0, :, pl.ds(r * width, width)], pan.at[r], load_sem.at[2 + r]))
    for load in loads:
        load.start()

    greeted = 3 + has_up.astype(jnp.int32) + has_down.astype(jnp.int32)
    pl.semaphore_wait(barrier, greeted + at_end.astype(jnp.int32) if direct else greeted)

    sent = []

    def send(src, dst, sem, device, guards=()):
        slot = len(sent)

        def make():
            return pltpu.make_async_remote_copy(
                src_ref=src(), dst_ref=dst(), send_sem=send_sem.at[slot], recv_sem=sem(),
                device_id=device, device_id_type=MESH)

        sent.append((guards, make))
        make().start()

    def place(bx, by, bz):
        return lambda: buf.at[2 * bz + by, 2 * bx + c]

    def part(bx, by, bz, h):
        return lambda: buf.at[2 * bz + by, 2 * bx + c, pl.ds(h * half, half)]

    def part_mark(bx, by, bz, h):
        return lambda: own_sem.at[((2 * bz + by) * 2 + bx) * 2 + h]

    def share_mark(bx, by, bz):
        return lambda: sib_sem.at[(2 * bz + by) * 2 + bx]

    def arrive(dst, sem):
        pltpu.make_async_remote_copy(
            src_ref=dst, dst_ref=dst, send_sem=send_sem.at[0], recv_sem=sem,
            device_id=to_s, device_id_type=MESH).wait_recv()

    def forward(bx, by, bz, h, device, guards=(), src=None):
        send(src or part(bx, by, bz, h), part(bx, by, bz, h), part_mark(bx, by, bz, h), device, guards)

    def share(bx, by, bz, guards=(), src=None):
        send(src or place(bx, by, bz), place(bx, by, bz), share_mark(bx, by, bz), to_s, guards)

    def take(bx, by, bz, h):
        arrive(part(bx, by, bz, h)(), part_mark(bx, by, bz, h)())

    def when(guard, body):
        pl.when(guard)(body)

    for h in HALVES:
        mine = lambda h=h: cur_ref.at[pl.ds(h * half, half)]
        when(has_up, lambda: forward(x, y, z, h, to_up, (has_up,), mine))
        when(has_down, lambda: forward(x, y, z, h, to_down, (has_down,), mine))
        if direct:
            when(at_end, lambda: forward(x, y, z, h, to_end, (at_end,), mine))
        forward(x, y, z, h, to_x, src=mine)
        forward(x, y, z, h, to_y, src=mine)
    share(x, y, z, src=lambda: cur_ref)

    acc[...] = jnp.zeros_like(acc)

    def go_on(bx, by, bz, h, up, guard):
        g, device = (has_up, to_up) if up else (has_down, to_down)
        when(g, lambda: forward(bx, by, bz, h, device, (guard, g)))

    def at_plane(up, d):
        return (z - d, z >= d) if up else (z + d, z + d < planes)

    def column(up, d, h):
        bz, guard = at_plane(up, d)

        def body():
            take(x, y, bz, h)
            if d < planes - (2 if direct else 1):
                go_on(x, y, bz, h, up, guard)
            forward(x, y, bz, h, to_x, (guard,))
            forward(x, y, bz, h, to_y, (guard,))
            if h == 1:
                share(x, y, bz, (guard,))

        when(guard, body)

    last = planes - 1 if planes >= 3 else planes

    def diagonal(up, d, h):
        bz, guard = at_plane(up, d)

        def body():
            take(nx, ny, bz, h)
            if d + 1 < last or (d + 1 == last and h == 1 and last < planes):
                go_on(nx, ny, bz, h, up, guard)
            if h == 1:
                share(nx, ny, bz, (guard,))

        when(guard, body)

    def side(bz, guards, over_x, over_y):
        take(nx, y, bz, 0)
        if over_y:
            forward(nx, y, bz, 0, to_y, guards)
        take(x, ny, bz, 0)
        take(x, ny, bz, 1)
        if over_x:
            forward(x, ny, bz, 1, to_x, guards)
        take(nx, y, bz, 1)
        share(nx, y, bz, guards)
        share(x, ny, bz, guards)

    def sides(up, d, h):
        bz, guard = at_plane(up, d)
        if h == 0:
            when(guard, lambda: side(bz, (guard,), False, d == last))

    def multiply(by, bz):
        for bx in (0, 1):
            arrive(buf.at[2 * bz + by, 2 * bx + 1 - c], share_mark(bx, by, bz)())
        r = 2 * bz + by
        lhs = buf[r].reshape(-1, width)
        acc[pl.ds(PAD, lhs.shape[0]), :] += lax.dot_general(
            lhs, pan[r], (((1,), (1,)), ((), ())), preferred_element_type=jnp.float32)

    def multiply_rows(by, bz, bx):
        arrive(buf.at[2 * bz + by, 2 * bx + 1 - c], share_mark(bx, by, bz)())
        r = 2 * bz + by
        lhs = buf[r, pl.ds(2 * bx, 2)].reshape(-1, width)
        at = pl.ds(pl.multiple_of(PAD + 2 * steps * bx, 8), 2 * steps)
        acc[at, :] += lax.dot_general(
            lhs, pan[r], (((1,), (1,)), ((), ())), preferred_element_type=jnp.float32)

    def multiply_own(up, d, h):
        bz, guard = at_plane(up, d)
        if h == 0:
            when(guard, lambda: multiply_rows(ny, bz, x))

    def multiply_other(up, d, h):
        bz, guard = at_plane(up, d)
        if h == 0:
            when(guard, lambda: multiply_rows(ny, bz, nx))

    def multiply_near(up, d, h):
        bz, guard = at_plane(up, d)
        if h == 0:
            when(guard, lambda: multiply(y, bz))

    def multiply_far(up, d, h):
        bz, guard = at_plane(up, d)
        if h == 0:
            when(guard, lambda: multiply(ny, bz))

    def both(step, d):
        if 1 <= d < planes:
            for h in HALVES:
                step(True, d, h)
                step(False, d, h)

    side(z, (), True, True)
    both(column, 1)
    for d in range(2, planes):
        both(column, d)
    for h in HALVES:
        take(nx, ny, z, h)
        when(has_up, lambda: forward(nx, ny, z, h, to_up, (has_up,)))
        when(has_down, lambda: forward(nx, ny, z, h, to_down, (has_down,)))
    share(nx, ny, z)
    if last > 1:
        both(diagonal, 1)
    for load in loads:
        load.wait()
    multiply(y, z)
    both(sides, 1)
    multiply(ny, z)
    for d in range(2, last):
        both(diagonal, d)
    for d in range(2, planes):
        both(sides, d)
        both(multiply_near, d - 1)
        both(multiply_far, d - 1)
    if planes > 1:
        both(multiply_near, planes - 1)
        both(multiply_own, planes - 1)
        if last < planes:
            both(diagonal, last)
        both(multiply_other, planes - 1)

    piece = steps // PIECES

    def shifted(bx, core, p):
        first = pl.multiple_of(PAD - 8 + (2 * bx + core) * steps + p * piece, 8)
        window = acc[pl.ds(first, piece + 8), :]
        return pltpu.roll(window, piece + lag, 0)[:piece]

    def give_piece(j, p):
        give[j, p] = shifted(nx if j == 0 else x, 1 - c, p)
        send(lambda j=j, p=p: give.at[j, p], lambda j=j, p=p: got.at[j, p],
             lambda j=j, p=p: give_sem.at[j * PIECES + p], to_s)

    def finish(group):
        for guards, make in group:
            if guards:
                g = functools.reduce(jnp.logical_and, guards)
                pl.when(g)(lambda make=make: make().wait_send())
            else:
                make().wait_send()

    gathered = len(sent)
    for p in range(PIECES):
        give_piece(0, p)
    for p in range(PIECES):
        arrive(got.at[0, p], give_sem.at[p])
        over[p] = shifted(nx, c, p) + got[0, p]
        send(lambda p=p: over.at[p], lambda p=p: landed.at[p], lambda p=p: over_sem.at[p], to_x)
    for p in range(PIECES):
        give_piece(1, p)
    finish(sent[:gathered])
    for p in range(PIECES):
        arrive(got.at[1, p], give_sem.at[PIECES + p])
        at = pl.ds(p * piece, piece)
        exc[at, :] = exc[at, :] - (shifted(x, c, p) + got[1, p])
    for p in range(PIECES):
        arrive(landed.at[p], over_sem.at[p])
        at = pl.ds(p * piece, piece)
        out_ref[at, :] = exc[at, :] - landed[p]

    finish(sent[gathered:])


def fused(currents, panels, excitation):
    steps, width = currents.shape
    count = panels.shape[1]
    lags, rows = lax.axis_size("lag"), lax.axis_size("row")
    planes = rows // 2
    hbm_spec = pl.BlockSpec(memory_space=pltpu.HBM)
    dma = pltpu.SemaphoreType.DMA
    piece = steps // PIECES
    return pl.pallas_call(
        functools.partial(kernel, planes),
        out_shape=jax.ShapeDtypeStruct(excitation.shape, jnp.float32),
        in_specs=[hbm_spec] * 3,
        out_specs=pl.BlockSpec(memory_space=pltpu.VMEM),
        scratch_shapes=[
            pltpu.VMEM((rows, lags, steps, width), jnp.bfloat16),
            pltpu.VMEM((rows, count, width), jnp.bfloat16),
            pltpu.VMEM((steps, count), jnp.float32),
            pltpu.VMEM((PAD + lags * steps, count), jnp.float32),
            pltpu.VMEM((2, PIECES, piece, count), jnp.float32),
            pltpu.VMEM((2, PIECES, piece, count), jnp.float32),
            pltpu.VMEM((PIECES, piece, count), jnp.float32),
            pltpu.VMEM((PIECES, piece, count), jnp.float32),
            dma((26 + 32 * planes + 3 * PIECES,)),
            dma((4 * rows,)),
            dma((2 * rows,)),
            dma((2 + rows,)),
            dma((2 * PIECES,)),
            dma((PIECES,)),
        ],
        compiler_params=pltpu.CompilerParams(
            collective_id=0, has_side_effects=True, vmem_limit_bytes=64 * 2**20),
        cost_estimate=pl.CostEstimate(
            flops=2 * lags * steps * width * rows * count,
            bytes_accessed=panels.size * 2, transcendentals=0),
    )(currents, panels, excitation)


def plain(currents, panels, excitation):
    gathered = lax.all_gather(currents, "row", axis=1, tiled=True)
    block_len = currents.shape[0]
    lag_total = lax.axis_size("lag")
    lag_index = lax.axis_index("lag")
    all_times = block_len * lag_total
    running = jnp.zeros((all_times + lag_total, panels.shape[1]), jnp.float32)
    product = lax.dot_general(
        lax.all_gather(gathered, "lag", axis=0, tiled=True),
        panels[0],
        (((1,), (1,)), ((), ())),
        preferred_element_type=jnp.float32,
    )
    running = lax.dynamic_update_slice_in_dim(running, product, lag_index, 0)
    field = lax.psum_scatter(running[:all_times], "lag", scatter_dimension=0, tiled=True)
    return excitation - field


def solution(mesh):
    paired = mesh.shape["lag"] == 4 and mesh.shape["row"] % 2 == 0
    return jax.shard_map(
        fused if paired else plain,
        mesh=mesh,
        in_specs=(P("lag", "row"), P("lag", "row", None), P("lag", "row")),
        out_specs=P("lag", "row"),
        check_vma=False,
    )
```

```python
import functools

import jax
import jax.numpy as jnp
from jax import lax
from jax.experimental import pallas as pl
from jax.experimental.pallas import tpu as pltpu
from jax.sharding import PartitionSpec as P

MESH = pl.DeviceIdType.MESH
PAD = 16
PIECES = 4
HALVES = (0, 1)


def kernel(planes, cur_ref, pan_ref, exc_ref, out_ref, buf, pan, exc, acc, give, got, over, landed,
           send_sem, own_sem, sib_sem, load_sem, give_sem, over_sem, store_sem):
    lag, row = lax.axis_index("lag"), lax.axis_index("row")
    x, c = lag // 2, lag % 2
    z, y = row // 2, row % 2
    nx, ny = 1 - x, 1 - y
    steps, width = cur_ref.shape
    rows = 2 * planes
    half = steps // 2
    to_x, to_y = (2 * nx + c, row), (lag, 2 * z + ny)
    to_s = (2 * x + 1 - c, row)
    to_up, to_down = (lag, row + 2), (lag, row - 2)
    has_up, has_down = z + 1 < planes, z >= 1
    direct = planes >= 4
    at_end = jnp.logical_or(z == 0, z == planes - 1)
    to_end = (lag, 2 * (planes - 1 - z) + y)

    barrier = pltpu.get_barrier_semaphore()

    def greet(device):
        pl.semaphore_signal(barrier, inc=1, device_id=device, device_id_type=MESH)

    greet(to_s)
    greet(to_x)
    greet(to_y)
    pl.when(has_up)(lambda: greet(to_up))
    pl.when(has_down)(lambda: greet(to_down))
    if direct:
        pl.when(at_end)(lambda: greet(to_end))

    loads = [pltpu.make_async_copy(cur_ref, buf.at[row, lag], load_sem.at[0]),
             pltpu.make_async_copy(exc_ref, exc, load_sem.at[1])]
    for r in range(rows):
        loads.append(pltpu.make_async_copy(
            pan_ref.at[0, :, pl.ds(r * width, width)], pan.at[r], load_sem.at[2 + r]))
    for load in loads:
        load.start()

    greeted = 3 + has_up.astype(jnp.int32) + has_down.astype(jnp.int32)
    pl.semaphore_wait(barrier, greeted + at_end.astype(jnp.int32) if direct else greeted)

    sent = []

    def send(src, dst, sem, device, guards=()):
        slot = len(sent)

        def make():
            return pltpu.make_async_remote_copy(
                src_ref=src(), dst_ref=dst(), send_sem=send_sem.at[slot], recv_sem=sem(),
                device_id=device, device_id_type=MESH)

        sent.append((guards, make))
        make().start()

    def place(bx, by, bz):
        return lambda: buf.at[2 * bz + by, 2 * bx + c]

    def part(bx, by, bz, h):
        return lambda: buf.at[2 * bz + by, 2 * bx + c, pl.ds(h * half, half)]

    def part_mark(bx, by, bz, h):
        return lambda: own_sem.at[((2 * bz + by) * 2 + bx) * 2 + h]

    def share_mark(bx, by, bz):
        return lambda: sib_sem.at[(2 * bz + by) * 2 + bx]

    def arrive(dst, sem):
        pltpu.make_async_remote_copy(
            src_ref=dst, dst_ref=dst, send_sem=send_sem.at[0], recv_sem=sem,
            device_id=to_s, device_id_type=MESH).wait_recv()

    def forward(bx, by, bz, h, device, guards=(), src=None):
        send(src or part(bx, by, bz, h), part(bx, by, bz, h), part_mark(bx, by, bz, h), device, guards)

    def share(bx, by, bz, guards=(), src=None):
        send(src or place(bx, by, bz), place(bx, by, bz), share_mark(bx, by, bz), to_s, guards)

    def take(bx, by, bz, h):
        arrive(part(bx, by, bz, h)(), part_mark(bx, by, bz, h)())

    def when(guard, body):
        pl.when(guard)(body)

    for h in HALVES:
        mine = lambda h=h: cur_ref.at[pl.ds(h * half, half)]
        when(has_up, lambda: forward(x, y, z, h, to_up, (has_up,), mine))
        when(has_down, lambda: forward(x, y, z, h, to_down, (has_down,), mine))
        forward(x, y, z, h, to_x, src=mine)
        forward(x, y, z, h, to_y, src=mine)
        if direct:
            when(at_end, lambda: forward(x, y, z, h, to_end, (at_end,), mine))
    share(x, y, z, src=lambda: cur_ref)

    acc[...] = jnp.zeros_like(acc)

    def go_on(bx, by, bz, h, up, guard):
        g, device = (has_up, to_up) if up else (has_down, to_down)
        when(g, lambda: forward(bx, by, bz, h, device, (guard, g)))

    def at_plane(up, d):
        return (z - d, z >= d) if up else (z + d, z + d < planes)

    def column(up, d, h):
        bz, guard = at_plane(up, d)

        def body():
            take(x, y, bz, h)
            if d < planes - (2 if direct else 1):
                go_on(x, y, bz, h, up, guard)
            forward(x, y, bz, h, to_x, (guard,))
            forward(x, y, bz, h, to_y, (guard,))
            if h == 1:
                share(x, y, bz, (guard,))

        when(guard, body)

    last = planes - 1 if planes >= 3 else planes

    def diagonal(up, d, h):
        bz, guard = at_plane(up, d)

        def body():
            take(nx, ny, bz, h)
            if d + 1 < last or (d + 1 == last and h == 1 and last < planes):
                go_on(nx, ny, bz, h, up, guard)
            if h == 1:
                share(nx, ny, bz, (guard,))

        when(guard, body)

    def side(bz, guards, over_x, over_y):
        take(nx, y, bz, 0)
        if over_y:
            forward(nx, y, bz, 0, to_y, guards)
        take(x, ny, bz, 0)
        take(x, ny, bz, 1)
        if over_x:
            forward(x, ny, bz, 1, to_x, guards)
        take(nx, y, bz, 1)
        share(nx, y, bz, guards)
        share(x, ny, bz, guards)

    def sides(up, d, h):
        bz, guard = at_plane(up, d)
        if h == 0:
            when(guard, lambda: side(bz, (guard,), False, d == last))

    def multiply(by, bz):
        for bx in (0, 1):
            arrive(buf.at[2 * bz + by, 2 * bx + 1 - c], share_mark(bx, by, bz)())
        r = 2 * bz + by
        lhs = buf[r].reshape(-1, width)
        acc[pl.ds(PAD, lhs.shape[0]), :] += lax.dot_general(
            lhs, pan[r], (((1,), (1,)), ((), ())), preferred_element_type=jnp.float32)

    def multiply_near(up, d, h):
        bz, guard = at_plane(up, d)
        if h == 0:
            when(guard, lambda: multiply(y, bz))

    def multiply_far(up, d, h):
        bz, guard = at_plane(up, d)
        if h == 0:
            when(guard, lambda: multiply(ny, bz))

    def both(step, d):
        if 1 <= d < planes:
            for h in HALVES:
                step(True, d, h)
                step(False, d, h)

    side(z, (), True, True)
    both(column, 1)
    both(column, 2)
    for h in HALVES:
        take(nx, ny, z, h)
        when(has_up, lambda: forward(nx, ny, z, h, to_up, (has_up,)))
        when(has_down, lambda: forward(nx, ny, z, h, to_down, (has_down,)))
    share(nx, ny, z)
    if last > 1:
        both(diagonal, 1)
    for load in loads:
        load.wait()
    multiply(y, z)
    both(column, 3)
    multiply(ny, z)
    both(sides, 1)
    both(multiply_near, 1)
    if last > 2:
        both(diagonal, 2)
    if last > 1:
        both(multiply_far, 1)
    for d in range(2, planes):
        if d + 2 < planes:
            both(column, d + 2)
        if 2 < d + 1 < last:
            both(diagonal, d + 1)
        if d < last or d == 2:
            both(sides, d)
        if d < last:
            if d + 1 == last:
                both(sides, d + 1)
            both(multiply_near, d)
            both(multiply_far, d)
        else:
            both(multiply_near, d)
            both(diagonal, d)
            both(multiply_far, d)

    piece = steps // PIECES

    def shifted(bx, core, p):
        first = pl.multiple_of(PAD - 8 + (2 * bx + core) * steps + p * piece, 8)
        window = acc[pl.ds(first, piece + 8), :]
        return pltpu.roll(window, piece + lag, 0)[:piece]

    def give_piece(j, p):
        give[j, p] = shifted(nx if j == 0 else x, 1 - c, p)
        send(lambda j=j, p=p: give.at[j, p], lambda j=j, p=p: got.at[j, p],
             lambda j=j, p=p: give_sem.at[j * PIECES + p], to_s)

    def finish(group):
        for guards, make in group:
            if guards:
                g = functools.reduce(jnp.logical_and, guards)
                pl.when(g)(lambda make=make: make().wait_send())
            else:
                make().wait_send()

    gathered = len(sent)
    for p in range(PIECES):
        give_piece(0, p)
    for p in range(PIECES):
        arrive(got.at[0, p], give_sem.at[p])
        over[p] = shifted(nx, c, p) + got[0, p]
        send(lambda p=p: over.at[p], lambda p=p: landed.at[p], lambda p=p: over_sem.at[p], to_x)
    for p in range(PIECES):
        give_piece(1, p)
    finish(sent[:gathered])
    for p in range(PIECES):
        arrive(got.at[1, p], give_sem.at[PIECES + p])
        at = pl.ds(p * piece, piece)
        exc[at, :] = exc[at, :] - (shifted(x, c, p) + got[1, p])
    stores = []
    for p in range(PIECES):
        arrive(landed.at[p], over_sem.at[p])
        at = pl.ds(p * piece, piece)
        exc[at, :] = exc[at, :] - landed[p]
        stores.append(pltpu.make_async_copy(exc.at[at], out_ref.at[at], store_sem.at[p]))
        stores[-1].start()

    finish(sent[gathered:])
    for store in stores:
        store.wait()


def fused(currents, panels, excitation):
    steps, width = currents.shape
    count = panels.shape[1]
    lags, rows = lax.axis_size("lag"), lax.axis_size("row")
    planes = rows // 2
    hbm_spec = pl.BlockSpec(memory_space=pltpu.HBM)
    dma = pltpu.SemaphoreType.DMA
    piece = steps // PIECES
    return pl.pallas_call(
        functools.partial(kernel, planes),
        out_shape=jax.ShapeDtypeStruct(excitation.shape, jnp.float32),
        in_specs=[hbm_spec] * 3,
        out_specs=hbm_spec,
        scratch_shapes=[
            pltpu.VMEM((rows, lags, steps, width), jnp.bfloat16),
            pltpu.VMEM((rows, count, width), jnp.bfloat16),
            pltpu.VMEM((steps, count), jnp.float32),
            pltpu.VMEM((PAD + lags * steps, count), jnp.float32),
            pltpu.VMEM((2, PIECES, piece, count), jnp.float32),
            pltpu.VMEM((2, PIECES, piece, count), jnp.float32),
            pltpu.VMEM((PIECES, piece, count), jnp.float32),
            pltpu.VMEM((PIECES, piece, count), jnp.float32),
            dma((26 + 32 * planes + 3 * PIECES,)),
            dma((4 * rows,)),
            dma((2 * rows,)),
            dma((2 + rows,)),
            dma((2 * PIECES,)),
            dma((PIECES,)),
            dma((PIECES,)),
        ],
        compiler_params=pltpu.CompilerParams(
            collective_id=0, has_side_effects=True, vmem_limit_bytes=64 * 2**20),
        cost_estimate=pl.CostEstimate(
            flops=2 * lags * steps * width * rows * count,
            bytes_accessed=panels.size * 2, transcendentals=0),
    )(currents, panels, excitation)


def plain(currents, panels, excitation):
    gathered = lax.all_gather(currents, "row", axis=1, tiled=True)
    block_len = currents.shape[0]
    lag_total = lax.axis_size("lag")
    lag_index = lax.axis_index("lag")
    all_times = block_len * lag_total
    running = jnp.zeros((all_times + lag_total, panels.shape[1]), jnp.float32)
    product = lax.dot_general(
        lax.all_gather(gathered, "lag", axis=0, tiled=True),
        panels[0],
        (((1,), (1,)), ((), ())),
        preferred_element_type=jnp.float32,
    )
    running = lax.dynamic_update_slice_in_dim(running, product, lag_index, 0)
    field = lax.psum_scatter(running[:all_times], "lag", scatter_dimension=0, tiled=True)
    return excitation - field


def solution(mesh):
    paired = mesh.shape["lag"] == 4 and mesh.shape["row"] % 2 == 0
    return jax.shard_map(
        fused if paired else plain,
        mesh=mesh,
        in_specs=(P("lag", "row"), P("lag", "row", None), P("lag", "row")),
        out_specs=P("lag", "row"),
        check_vma=False,
    )
```

```python
import functools

import jax
import jax.numpy as jnp
from jax import lax
from jax.experimental import pallas as pl
from jax.experimental.pallas import tpu as pltpu
from jax.sharding import PartitionSpec as P

MESH = pl.DeviceIdType.MESH
PAD = 16
PIECES = 4
HALVES = (0, 1)


def kernel(planes, cur_ref, pan_ref, exc_ref, out_ref, buf, pan, exc, acc, give, got, over, landed,
           send_sem, own_sem, sib_sem, load_sem, give_sem, over_sem, store_sem):
    lag, row = lax.axis_index("lag"), lax.axis_index("row")
    x, c = lag // 2, lag % 2
    z, y = row // 2, row % 2
    nx, ny = 1 - x, 1 - y
    steps, width = cur_ref.shape
    rows = 2 * planes
    half = steps // 2
    to_x, to_y = (2 * nx + c, row), (lag, 2 * z + ny)
    to_s = (2 * x + 1 - c, row)
    to_up, to_down = (lag, row + 2), (lag, row - 2)
    has_up, has_down = z + 1 < planes, z >= 1
    direct = planes >= 4
    at_end = jnp.logical_or(z == 0, z == planes - 1)
    to_end = (lag, 2 * (planes - 1 - z) + y)

    barrier = pltpu.get_barrier_semaphore()

    def greet(device):
        pl.semaphore_signal(barrier, inc=1, device_id=device, device_id_type=MESH)

    greet(to_s)
    greet(to_x)
    greet(to_y)
    pl.when(has_up)(lambda: greet(to_up))
    pl.when(has_down)(lambda: greet(to_down))
    if direct:
        pl.when(at_end)(lambda: greet(to_end))

    loads = [pltpu.make_async_copy(cur_ref, buf.at[row, lag], load_sem.at[0]),
             pltpu.make_async_copy(exc_ref, exc, load_sem.at[1])]
    for r in range(rows):
        loads.append(pltpu.make_async_copy(
            pan_ref.at[0, :, pl.ds(r * width, width)], pan.at[r], load_sem.at[2 + r]))
    for load in loads:
        load.start()

    greeted = 3 + has_up.astype(jnp.int32) + has_down.astype(jnp.int32)
    pl.semaphore_wait(barrier, greeted + at_end.astype(jnp.int32) if direct else greeted)

    sent = []

    def send(src, dst, sem, device, guards=()):
        slot = len(sent)

        def make():
            return pltpu.make_async_remote_copy(
                src_ref=src(), dst_ref=dst(), send_sem=send_sem.at[slot], recv_sem=sem(),
                device_id=device, device_id_type=MESH)

        sent.append((guards, make))
        make().start()

    def place(bx, by, bz):
        return lambda: buf.at[2 * bz + by, 2 * bx + c]

    def part(bx, by, bz, h):
        return lambda: buf.at[2 * bz + by, 2 * bx + c, pl.ds(h * half, half)]

    def part_mark(bx, by, bz, h):
        return lambda: own_sem.at[((2 * bz + by) * 2 + bx) * 2 + h]

    def share_mark(bx, by, bz):
        return lambda: sib_sem.at[(2 * bz + by) * 2 + bx]

    def arrive(dst, sem):
        pltpu.make_async_remote_copy(
            src_ref=dst, dst_ref=dst, send_sem=send_sem.at[0], recv_sem=sem,
            device_id=to_s, device_id_type=MESH).wait_recv()

    def forward(bx, by, bz, h, device, guards=(), src=None):
        send(src or part(bx, by, bz, h), part(bx, by, bz, h), part_mark(bx, by, bz, h), device, guards)

    def share(bx, by, bz, guards=(), src=None):
        send(src or place(bx, by, bz), place(bx, by, bz), share_mark(bx, by, bz), to_s, guards)

    def take(bx, by, bz, h):
        arrive(part(bx, by, bz, h)(), part_mark(bx, by, bz, h)())

    def when(guard, body):
        pl.when(guard)(body)

    for h in HALVES:
        mine = lambda h=h: cur_ref.at[pl.ds(h * half, half)]
        when(has_up, lambda: forward(x, y, z, h, to_up, (has_up,), mine))
        when(has_down, lambda: forward(x, y, z, h, to_down, (has_down,), mine))
        forward(x, y, z, h, to_x, src=mine)
        forward(x, y, z, h, to_y, src=mine)
        if direct:
            when(at_end, lambda: forward(x, y, z, h, to_end, (at_end,), mine))
    share(x, y, z, src=lambda: cur_ref)

    acc[...] = jnp.zeros_like(acc)

    def go_on(bx, by, bz, h, up, guard):
        g, device = (has_up, to_up) if up else (has_down, to_down)
        when(g, lambda: forward(bx, by, bz, h, device, (guard, g)))

    def at_plane(up, d):
        return (z - d, z >= d) if up else (z + d, z + d < planes)

    def column(up, d, h):
        bz, guard = at_plane(up, d)

        def body():
            take(x, y, bz, h)
            if d < planes - (2 if direct else 1):
                go_on(x, y, bz, h, up, guard)
            forward(x, y, bz, h, to_x, (guard,))
            forward(x, y, bz, h, to_y, (guard,))
            if h == 1:
                share(x, y, bz, (guard,))

        when(guard, body)

    last = planes - 1 if planes >= 3 else planes

    def diagonal(up, d, h):
        bz, guard = at_plane(up, d)

        def body():
            take(nx, ny, bz, h)
            if d + 1 < last:
                go_on(nx, ny, bz, h, up, guard)
            if h == 1:
                share(nx, ny, bz, (guard,))

        when(guard, body)

    def side(bz, guards, over_x, over_y):
        take(nx, y, bz, 0)
        if over_y:
            forward(nx, y, bz, 0, to_y, guards)
        take(x, ny, bz, 0)
        take(x, ny, bz, 1)
        if over_x:
            forward(x, ny, bz, 1, to_x, guards)
        take(nx, y, bz, 1)
        share(nx, y, bz, guards)
        share(x, ny, bz, guards)

    def sides(up, d, h):
        bz, guard = at_plane(up, d)
        if h == 0:
            when(guard, lambda: side(bz, (guard,), d == last, d == last))

    def multiply(by, bz):
        for bx in (0, 1):
            arrive(buf.at[2 * bz + by, 2 * bx + 1 - c], share_mark(bx, by, bz)())
        r = 2 * bz + by
        lhs = buf[r].reshape(-1, width)
        acc[pl.ds(PAD, lhs.shape[0]), :] += lax.dot_general(
            lhs, pan[r], (((1,), (1,)), ((), ())), preferred_element_type=jnp.float32)

    def multiply_near(up, d, h):
        bz, guard = at_plane(up, d)
        if h == 0:
            when(guard, lambda: multiply(y, bz))

    def multiply_far(up, d, h):
        bz, guard = at_plane(up, d)
        if h == 0:
            when(guard, lambda: multiply(ny, bz))

    def both(step, d):
        if 1 <= d < planes:
            for h in HALVES:
                step(True, d, h)
                step(False, d, h)

    side(z, (), True, True)
    both(column, 1)
    both(column, 2)
    both(column, 3)
    for h in HALVES:
        take(nx, ny, z, h)
        when(has_up, lambda: forward(nx, ny, z, h, to_up, (has_up,)))
        when(has_down, lambda: forward(nx, ny, z, h, to_down, (has_down,)))
    share(nx, ny, z)
    if last > 1:
        both(diagonal, 1)
    for load in loads:
        load.wait()
    multiply(y, z)
    multiply(ny, z)
    both(sides, 1)
    both(multiply_near, 1)
    if last > 2:
        both(diagonal, 2)
    if last > 1:
        both(multiply_far, 1)
    for d in range(2, planes):
        if d + 2 < planes:
            both(column, d + 2)
        if 2 < d + 1 < last:
            both(diagonal, d + 1)
        if d < last or d == 2:
            both(sides, d)
        if d < last:
            if d + 1 == last:
                both(sides, d + 1)
            both(multiply_near, d)
            both(multiply_far, d)
        else:
            both(multiply_near, d)
            both(diagonal, d)
            both(multiply_far, d)

    piece = steps // PIECES

    def shifted(bx, core, p):
        first = pl.multiple_of(PAD - 8 + (2 * bx + core) * steps + p * piece, 8)
        window = acc[pl.ds(first, piece + 8), :]
        return pltpu.roll(window, piece + lag, 0)[:piece]

    def give_piece(j, p):
        give[j, p] = shifted(nx if j == 0 else x, 1 - c, p)
        send(lambda j=j, p=p: give.at[j, p], lambda j=j, p=p: got.at[j, p],
             lambda j=j, p=p: give_sem.at[j * PIECES + p], to_s)

    def finish(group):
        for guards, make in group:
            if guards:
                g = functools.reduce(jnp.logical_and, guards)
                pl.when(g)(lambda make=make: make().wait_send())
            else:
                make().wait_send()

    gathered = len(sent)
    for p in range(PIECES):
        give_piece(0, p)
    for p in range(PIECES):
        arrive(got.at[0, p], give_sem.at[p])
        over[p] = shifted(nx, c, p) + got[0, p]
        send(lambda p=p: over.at[p], lambda p=p: landed.at[p], lambda p=p: over_sem.at[p], to_x)
    for p in range(PIECES):
        give_piece(1, p)
    finish(sent[:gathered])
    for p in range(PIECES):
        arrive(got.at[1, p], give_sem.at[PIECES + p])
        at = pl.ds(p * piece, piece)
        exc[at, :] = exc[at, :] - (shifted(x, c, p) + got[1, p])
    stores = []
    for p in range(PIECES):
        arrive(landed.at[p], over_sem.at[p])
        at = pl.ds(p * piece, piece)
        exc[at, :] = exc[at, :] - landed[p]
        stores.append(pltpu.make_async_copy(exc.at[at], out_ref.at[at], store_sem.at[p]))
        stores[-1].start()

    finish(sent[gathered:])
    for store in stores:
        store.wait()


def fused(currents, panels, excitation):
    steps, width = currents.shape
    count = panels.shape[1]
    lags, rows = lax.axis_size("lag"), lax.axis_size("row")
    planes = rows // 2
    hbm_spec = pl.BlockSpec(memory_space=pltpu.HBM)
    dma = pltpu.SemaphoreType.DMA
    piece = steps // PIECES
    return pl.pallas_call(
        functools.partial(kernel, planes),
        out_shape=jax.ShapeDtypeStruct(excitation.shape, jnp.float32),
        in_specs=[hbm_spec] * 3,
        out_specs=hbm_spec,
        scratch_shapes=[
            pltpu.VMEM((rows, lags, steps, width), jnp.bfloat16),
            pltpu.VMEM((rows, count, width), jnp.bfloat16),
            pltpu.VMEM((steps, count), jnp.float32),
            pltpu.VMEM((PAD + lags * steps, count), jnp.float32),
            pltpu.VMEM((2, PIECES, piece, count), jnp.float32),
            pltpu.VMEM((2, PIECES, piece, count), jnp.float32),
            pltpu.VMEM((PIECES, piece, count), jnp.float32),
            pltpu.VMEM((PIECES, piece, count), jnp.float32),
            dma((26 + 32 * planes + 3 * PIECES,)),
            dma((4 * rows,)),
            dma((2 * rows,)),
            dma((2 + rows,)),
            dma((2 * PIECES,)),
            dma((PIECES,)),
            dma((PIECES,)),
        ],
        compiler_params=pltpu.CompilerParams(
            collective_id=0, has_side_effects=True, vmem_limit_bytes=64 * 2**20),
        cost_estimate=pl.CostEstimate(
            flops=2 * lags * steps * width * rows * count,
            bytes_accessed=panels.size * 2, transcendentals=0),
    )(currents, panels, excitation)


def plain(currents, panels, excitation):
    gathered = lax.all_gather(currents, "row", axis=1, tiled=True)
    block_len = currents.shape[0]
    lag_total = lax.axis_size("lag")
    lag_index = lax.axis_index("lag")
    all_times = block_len * lag_total
    running = jnp.zeros((all_times + lag_total, panels.shape[1]), jnp.float32)
    product = lax.dot_general(
        lax.all_gather(gathered, "lag", axis=0, tiled=True),
        panels[0],
        (((1,), (1,)), ((), ())),
        preferred_element_type=jnp.float32,
    )
    running = lax.dynamic_update_slice_in_dim(running, product, lag_index, 0)
    field = lax.psum_scatter(running[:all_times], "lag", scatter_dimension=0, tiled=True)
    return excitation - field


def solution(mesh):
    paired = mesh.shape["lag"] == 4 and mesh.shape["row"] % 2 == 0
    return jax.shard_map(
        fused if paired else plain,
        mesh=mesh,
        in_specs=(P("lag", "row"), P("lag", "row", None), P("lag", "row")),
        out_specs=P("lag", "row"),
        check_vma=False,
    )
```

```python
import functools

import jax
import jax.numpy as jnp
from jax import lax
from jax.experimental import pallas as pl
from jax.experimental.pallas import tpu as pltpu
from jax.sharding import PartitionSpec as P

MESH = pl.DeviceIdType.MESH
PAD = 16
PIECES = 4
HALVES = (0, 1)


def kernel(planes, cur_ref, pan_ref, exc_ref, out_ref, buf, pan, exc, acc, give, got, over, landed,
           send_sem, own_sem, sib_sem, load_sem, give_sem, over_sem, store_sem):
    lag, row = lax.axis_index("lag"), lax.axis_index("row")
    x, c = lag // 2, lag % 2
    z, y = row // 2, row % 2
    nx, ny = 1 - x, 1 - y
    steps, width = cur_ref.shape
    rows = 2 * planes
    half = steps // 2
    to_x, to_y = (2 * nx + c, row), (lag, 2 * z + ny)
    to_s = (2 * x + 1 - c, row)
    to_up, to_down = (lag, row + 2), (lag, row - 2)
    has_up, has_down = z + 1 < planes, z >= 1

    barrier = pltpu.get_barrier_semaphore()

    def greet(device):
        pl.semaphore_signal(barrier, inc=1, device_id=device, device_id_type=MESH)

    greet(to_s)
    greet(to_x)
    greet(to_y)
    pl.when(has_up)(lambda: greet(to_up))
    pl.when(has_down)(lambda: greet(to_down))

    loads = [pltpu.make_async_copy(cur_ref, buf.at[row, lag], load_sem.at[0]),
             pltpu.make_async_copy(exc_ref, exc, load_sem.at[1])]
    for r in range(rows):
        loads.append(pltpu.make_async_copy(
            pan_ref.at[0, :, pl.ds(r * width, width)], pan.at[r], load_sem.at[2 + r]))
    for load in loads:
        load.start()

    pl.semaphore_wait(barrier, 3 + has_up.astype(jnp.int32) + has_down.astype(jnp.int32))

    sent = []

    def send(src, dst, sem, device, guards=()):
        slot = len(sent)

        def make():
            return pltpu.make_async_remote_copy(
                src_ref=src(), dst_ref=dst(), send_sem=send_sem.at[slot], recv_sem=sem(),
                device_id=device, device_id_type=MESH)

        sent.append((guards, make))
        make().start()

    def place(bx, by, bz):
        return lambda: buf.at[2 * bz + by, 2 * bx + c]

    def part(bx, by, bz, h):
        return lambda: buf.at[2 * bz + by, 2 * bx + c, pl.ds(h * half, half)]

    def part_mark(bx, by, bz, h):
        return lambda: own_sem.at[((2 * bz + by) * 2 + bx) * 2 + h]

    def share_mark(bx, by, bz):
        return lambda: sib_sem.at[(2 * bz + by) * 2 + bx]

    def arrive(dst, sem):
        pltpu.make_async_remote_copy(
            src_ref=dst, dst_ref=dst, send_sem=send_sem.at[0], recv_sem=sem,
            device_id=to_s, device_id_type=MESH).wait_recv()

    def forward(bx, by, bz, h, device, guards=(), src=None):
        send(src or part(bx, by, bz, h), part(bx, by, bz, h), part_mark(bx, by, bz, h), device, guards)

    def share(bx, by, bz, guards=(), src=None):
        send(src or place(bx, by, bz), place(bx, by, bz), share_mark(bx, by, bz), to_s, guards)

    def take(bx, by, bz, h):
        arrive(part(bx, by, bz, h)(), part_mark(bx, by, bz, h)())

    def when(guard, body):
        pl.when(guard)(body)

    for h in HALVES:
        mine = lambda h=h: cur_ref.at[pl.ds(h * half, half)]
        when(has_up, lambda: forward(x, y, z, h, to_up, (has_up,), mine))
        when(has_down, lambda: forward(x, y, z, h, to_down, (has_down,), mine))
        forward(x, y, z, h, to_x, src=mine)
        forward(x, y, z, h, to_y, src=mine)
    share(x, y, z, src=lambda: cur_ref)

    acc[...] = jnp.zeros_like(acc)

    def go_on(bx, by, bz, h, up, guard):
        g, device = (has_up, to_up) if up else (has_down, to_down)
        when(g, lambda: forward(bx, by, bz, h, device, (guard, g)))

    def at_plane(up, d):
        return (z - d, z >= d) if up else (z + d, z + d < planes)

    def column(up, d, h):
        bz, guard = at_plane(up, d)

        def body():
            take(x, y, bz, h)
            if d < planes - 1:
                go_on(x, y, bz, h, up, guard)
            forward(x, y, bz, h, to_x, (guard,))
            forward(x, y, bz, h, to_y, (guard,))
            if h == 1:
                share(x, y, bz, (guard,))

        when(guard, body)

    last = planes - 1 if planes >= 3 else planes

    def diagonal(up, d, h):
        bz, guard = at_plane(up, d)

        def body():
            take(nx, ny, bz, h)
            if d + 1 < last or (d + 1 == last and h == 1 and last < planes):
                go_on(nx, ny, bz, h, up, guard)
            if h == 1:
                share(nx, ny, bz, (guard,))

        when(guard, body)

    def side(bz, guards, over_x, over_y):
        take(nx, y, bz, 0)
        if over_y:
            forward(nx, y, bz, 0, to_y, guards)
        take(x, ny, bz, 0)
        take(x, ny, bz, 1)
        if over_x:
            forward(x, ny, bz, 1, to_x, guards)
        take(nx, y, bz, 1)
        share(nx, y, bz, guards)
        share(x, ny, bz, guards)

    def sides(up, d, h):
        bz, guard = at_plane(up, d)
        if h == 0:
            when(guard, lambda: side(bz, (guard,), False, d == last))

    def multiply(by, bz):
        for bx in (0, 1):
            arrive(buf.at[2 * bz + by, 2 * bx + 1 - c], share_mark(bx, by, bz)())
        r = 2 * bz + by
        lhs = buf[r].reshape(-1, width)
        acc[pl.ds(PAD, lhs.shape[0]), :] += lax.dot_general(
            lhs, pan[r], (((1,), (1,)), ((), ())), preferred_element_type=jnp.float32)

    def multiply_near(up, d, h):
        bz, guard = at_plane(up, d)
        if h == 0:
            when(guard, lambda: multiply(y, bz))

    def multiply_far(up, d, h):
        bz, guard = at_plane(up, d)
        if h == 0:
            when(guard, lambda: multiply(ny, bz))

    def both(step, d):
        if 1 <= d < planes:
            for h in HALVES:
                step(True, d, h)
                step(False, d, h)

    side(z, (), True, True)
    both(column, 1)
    both(column, 2)
    for h in HALVES:
        take(nx, ny, z, h)
        when(has_up, lambda: forward(nx, ny, z, h, to_up, (has_up,)))
        when(has_down, lambda: forward(nx, ny, z, h, to_down, (has_down,)))
    share(nx, ny, z)
    if last > 1:
        both(diagonal, 1)
    for load in loads:
        load.wait()
    multiply(y, z)
    both(column, 3)
    multiply(ny, z)
    both(sides, 1)
    both(multiply_near, 1)
    if last > 2:
        both(diagonal, 2)
    if last > 1:
        both(multiply_far, 1)
    for d in range(2, planes):
        if d + 2 < planes:
            both(column, d + 2)
        if 2 < d + 1 < last:
            both(diagonal, d + 1)
        if d < last or d == 2:
            both(sides, d)
        if d < last:
            if d + 1 == last:
                both(sides, d + 1)
            both(multiply_near, d)
            both(multiply_far, d)
        else:
            both(multiply_near, d)
            both(diagonal, d)
            both(multiply_far, d)

    piece = steps // PIECES

    def shifted(bx, core, p):
        first = pl.multiple_of(PAD - 8 + (2 * bx + core) * steps + p * piece, 8)
        window = acc[pl.ds(first, piece + 8), :]
        return pltpu.roll(window, piece + lag, 0)[:piece]

    def give_piece(j, p):
        give[j, p] = shifted(nx if j == 0 else x, 1 - c, p)
        send(lambda j=j, p=p: give.at[j, p], lambda j=j, p=p: got.at[j, p],
             lambda j=j, p=p: give_sem.at[j * PIECES + p], to_s)

    def finish(group):
        for guards, make in group:
            if guards:
                g = functools.reduce(jnp.logical_and, guards)
                pl.when(g)(lambda make=make: make().wait_send())
            else:
                make().wait_send()

    gathered = len(sent)
    for p in range(PIECES):
        give_piece(0, p)
    for p in range(PIECES):
        arrive(got.at[0, p], give_sem.at[p])
        over[p] = shifted(nx, c, p) + got[0, p]
        send(lambda p=p: over.at[p], lambda p=p: landed.at[p], lambda p=p: over_sem.at[p], to_x)
    for p in range(PIECES):
        give_piece(1, p)
    finish(sent[:gathered])
    for p in range(PIECES):
        arrive(got.at[1, p], give_sem.at[PIECES + p])
        at = pl.ds(p * piece, piece)
        exc[at, :] = exc[at, :] - (shifted(x, c, p) + got[1, p])
    stores = []
    for p in range(PIECES):
        arrive(landed.at[p], over_sem.at[p])
        at = pl.ds(p * piece, piece)
        exc[at, :] = exc[at, :] - landed[p]
        stores.append(pltpu.make_async_copy(exc.at[at], out_ref.at[at], store_sem.at[p]))
        stores[-1].start()

    finish(sent[gathered:])
    for store in stores:
        store.wait()


def fused(currents, panels, excitation):
    steps, width = currents.shape
    count = panels.shape[1]
    lags, rows = lax.axis_size("lag"), lax.axis_size("row")
    planes = rows // 2
    hbm_spec = pl.BlockSpec(memory_space=pltpu.HBM)
    dma = pltpu.SemaphoreType.DMA
    piece = steps // PIECES
    return pl.pallas_call(
        functools.partial(kernel, planes),
        out_shape=jax.ShapeDtypeStruct(excitation.shape, jnp.float32),
        in_specs=[hbm_spec] * 3,
        out_specs=hbm_spec,
        scratch_shapes=[
            pltpu.VMEM((rows, lags, steps, width), jnp.bfloat16),
            pltpu.VMEM((rows, count, width), jnp.bfloat16),
            pltpu.VMEM((steps, count), jnp.float32),
            pltpu.VMEM((PAD + lags * steps, count), jnp.float32),
            pltpu.VMEM((2, PIECES, piece, count), jnp.float32),
            pltpu.VMEM((2, PIECES, piece, count), jnp.float32),
            pltpu.VMEM((PIECES, piece, count), jnp.float32),
            pltpu.VMEM((PIECES, piece, count), jnp.float32),
            dma((26 + 32 * planes + 3 * PIECES,)),
            dma((4 * rows,)),
            dma((2 * rows,)),
            dma((2 + rows,)),
            dma((2 * PIECES,)),
            dma((PIECES,)),
            dma((PIECES,)),
        ],
        compiler_params=pltpu.CompilerParams(
            collective_id=0, has_side_effects=True, vmem_limit_bytes=64 * 2**20),
        cost_estimate=pl.CostEstimate(
            flops=2 * lags * steps * width * rows * count,
            bytes_accessed=panels.size * 2, transcendentals=0),
    )(currents, panels, excitation)


def plain(currents, panels, excitation):
    gathered = lax.all_gather(currents, "row", axis=1, tiled=True)
    block_len = currents.shape[0]
    lag_total = lax.axis_size("lag")
    lag_index = lax.axis_index("lag")
    all_times = block_len * lag_total
    running = jnp.zeros((all_times + lag_total, panels.shape[1]), jnp.float32)
    product = lax.dot_general(
        lax.all_gather(gathered, "lag", axis=0, tiled=True),
        panels[0],
        (((1,), (1,)), ((), ())),
        preferred_element_type=jnp.float32,
    )
    running = lax.dynamic_update_slice_in_dim(running, product, lag_index, 0)
    field = lax.psum_scatter(running[:all_times], "lag", scatter_dimension=0, tiled=True)
    return excitation - field


def solution(mesh):
    paired = mesh.shape["lag"] == 4 and mesh.shape["row"] % 2 == 0
    return jax.shard_map(
        fused if paired else plain,
        mesh=mesh,
        in_specs=(P("lag", "row"), P("lag", "row", None), P("lag", "row")),
        out_specs=P("lag", "row"),
        check_vma=False,
    )
```
